512 devices in a mesh: ops: 32 (over z, x), sec: 16 (over y, core).
Axes of the slice: x: 4, y: 8, z: 8, core: 2. Of those that a mesh axis runs over, the one named last changes fastest.
Arguments:
- psi: bfloat16 [64, 256, 256], P('sec'), may hold values from -6 to 6
- left_ops: bfloat16 [512, 256, 256], P('ops'), may hold values from -0.375 to 0.375
- right_ops: bfloat16 [512, 256, 256], P('ops'), may hold values from -0.375 to 0.375
- coef: float32 [512], P('ops'), may hold values from -1.25 to 1.25
- source: int32 [512, 64], P('ops', 'sec'), may hold values from 0 to 63
- active: int32 [512, 64], P('ops', 'sec'), may hold values from 0 to 1, as said below
- left_block: bfloat16 [64, 256, 256], P('sec'), may hold values from -0.375 to 0.375
- right_block: bfloat16 [64, 256, 256], P('sec'), may hold values from -0.375 to 0.375
Outputs:
- sigma: float32 [64, 256, 256], P('sec', 'ops')
The draws below stay inside these ranges and needn't reach their ends.
Inputs may be any that keep to these rules, and one draw needn't show every extreme that they name: active[k, t] is 0 or 1; each target sector t has its own rate, the same for all terms, between 1/32 and 1/2, so most pairs are inactive and sectors differ.
All inputs are finite; a program needn't handle non-finite values.
Results may differ from the reference program's by a relative error of at most 0.0023.
Values may be sent and summed in bfloat16 or wider, within the bound.
No kernel may reach another device: no remote copies, remote signals or barrier semaphores. Data moves between devices by JAX's collectives and lax.ppermute only.
A program may use at most 64 MiB of HBM per device.

```python
import jax
import jax.numpy as jnp
from jax import lax

TILE = 256
KTERMS = 512
NSEC = 64


def draw_active(key, part):
    key = jax.random.fold_in(key, 7)
    level_key, pick_key = jax.random.split(key)
    levels = jax.random.randint(level_key, (NSEC,), 0, 5)
    picks = jax.random.randint(pick_key, (KTERMS, NSEC), 0, 32)
    return (picks < jnp.left_shift(1, levels)[None, :]).astype(jnp.int32)


def with_ends(drawn, stream_key, low, largest):
    place = [jax.random.randint(jax.random.fold_in(stream_key, axis), (), 0, length) for axis, length in enumerate(drawn.shape)]
    main_axis = drawn.shape.index(max(drawn.shape))
    next_to = place[:main_axis] + [(place[main_axis] + 1) % drawn.shape[main_axis]] + place[main_axis + 1:]
    return drawn.at[tuple(place)].set(low).at[tuple(next_to)].set(largest)


def shard_levels(key, dims, cuts, low, top_value):
    factor_of, own = 1.0, jax.random.fold_in(key, 6)
    for axis_at, parts in cuts:
        heights = jnp.exp(jax.random.uniform(jax.random.fold_in(own, axis_at), (parts,), jnp.float32, low / len(cuts), top_value / len(cuts)))
        factor_of = factor_of * jnp.repeat(heights, dims[axis_at] // parts).reshape([-1 if axis == axis_at else 1 for axis in range(len(dims))])
    return factor_of


def noise(own_key, shape, scale, limit, pieces=(), dtype=jnp.bfloat16):
    level = shard_levels(own_key, shape, pieces, -0.22, 0.18) if pieces else 1.0
    drawn = jax.random.normal(own_key, shape, jnp.float32) * scale * level
    return jnp.minimum(jnp.maximum(drawn, -limit), limit).astype(dtype)


def setup_inputs(seed: int = 0) -> dict:
    key_list = jax.random.split(jax.random.key(seed), 9)
    return {
        "psi": noise(key_list[0], (NSEC, TILE, TILE), 1.0, 6.0, ((0, 16),)),
        "left_ops": noise(key_list[1], (KTERMS, TILE, TILE), TILE ** -0.5, 0.375, ((0, 32),)),
        "right_ops": noise(key_list[2], (KTERMS, TILE, TILE), TILE ** -0.5, 0.375, ((0, 32),)),
        "coef": noise(key_list[3], (KTERMS,), (2.0 / KTERMS ** 0.5), 1.25, ((0, 32),), jnp.float32),
        "source": with_ends(jax.random.randint(key_list[4], (KTERMS, NSEC), 0, NSEC), jax.random.fold_in(key_list[4], 1), 0, NSEC - 1).astype(jnp.int32),
        "active": draw_active(jax.random.fold_in(key_list[8], 71), 0),
        "left_block": noise(key_list[6], (NSEC, TILE, TILE), TILE ** -0.5, 0.375, ((0, 16),)),
        "right_block": noise(key_list[7], (NSEC, TILE, TILE), TILE ** -0.5, 0.375, ((0, 16),)),
    }


def reference(psi, left_ops, right_ops, coef, source, active, left_block, right_block):
    psi_wide = psi.astype(jnp.float32)
    weights = coef[:, None] * active.astype(jnp.float32)

    def one_term(total, packed):
        left_one, right_one, src_row, weight_row = packed
        mixed = jnp.einsum("ij,sjl->sil", left_one.astype(jnp.float32), psi_wide).astype(jnp.bfloat16)
        image = jnp.einsum("sil,lm->sim", mixed.astype(jnp.float32), right_one.astype(jnp.float32))
        picked = jnp.take(image, src_row.astype(jnp.int32), axis=0)
        return total + weight_row[:, None, None] * picked, None

    start = jnp.zeros(psi.shape, jnp.float32)
    terms, unused = lax.scan(one_term, start, (left_ops, right_ops, source, weights))
    local_part = jnp.einsum("tij,tjl->til", left_block.astype(jnp.float32), psi_wide)
    local_part = local_part + jnp.einsum("tij,tjl->til", psi_wide, right_block.astype(jnp.float32))
    return local_part + terms
```

```python
import functools

import jax
import jax.numpy as jnp
from jax import lax
from jax.experimental import pallas as pl
from jax.experimental.pallas import tpu as pltpu
from jax.sharding import Mesh, PartitionSpec as P

AXES = (8, 4, 8, 2)
NAMES = ("z", "x", "y", "core")
GROUP = 4

PLACES = ((0, 1, 0), (1, 4, 2), (-1, 5, 3), (2, 7, 6))


def places_of(codes, sec_dev, core, ring):
    source_core = (codes // sec_dev) % 2
    away = (codes // (2 * sec_dev) - ring) * jnp.where(source_core == 0, 1, -1)
    block = jnp.full_like(codes, -1)
    for far, other, own in PLACES:
        here = (away - far) % AXES[2] == 0
        block = jnp.where(here, jnp.where(source_core == core, own, other), block)
    held = jnp.logical_and(codes >= 0, block >= 0)
    return jnp.where(held, block * sec_dev + codes % sec_dev, 2 * len(PLACES) * sec_dev)


def plan_kernel(
    place_ref, coef_ref, left_hbm, right_hbm,
    list_ref, weight_ref, count_ref, left_ref, right_ref, start_ref, sems,
):
    copies = [
        pltpu.make_async_copy(left_hbm, left_ref, sems.at[0]),
        pltpu.make_async_copy(right_hbm, right_ref, sems.at[1]),
    ]
    for copy in copies:
        copy.start()
    pairs = place_ref.shape[0]
    sources = start_ref.shape[0] - 1
    targets = pairs // coef_ref.shape[0]

    def clear_start(s, carry):
        start_ref[s] = 0
        return carry

    def count(i, carry):
        place = place_ref[i]
        start_ref[place] = start_ref[place] + 1
        return carry

    def start_of(s, total):
        held = start_ref[s]
        start_ref[s] = total
        return total + held

    def put(i, carry):
        place = place_ref[i]
        at = start_ref[place]
        start_ref[place] = at + 1
        list_ref[at] = i + pairs * place
        weight_ref[at] = coef_ref[lax.div(i, targets)]
        return carry

    def clear(i, carry):
        list_ref[i] = 0
        weight_ref[i] = 0.0
        return carry

    lax.fori_loop(0, sources + 1, clear_start, 0)
    lax.fori_loop(0, pairs, count, 0)
    total = lax.fori_loop(0, sources, start_of, 0)
    start_ref[sources] = total
    lax.fori_loop(0, pairs, put, 0)
    lax.fori_loop(total, pairs + GROUP, clear, 0)
    count_ref[0] = total
    for copy in copies:
        copy.wait()


def add_kernel(parts_ref, out_ref):
    total = parts_ref[0].astype(jnp.float32)
    for i in range(1, parts_ref.shape[0]):
        total += parts_ref[i].astype(jnp.float32)
    out_ref[...] = total.astype(out_ref.dtype)


def terms_kernel(list_ref, weight_ref, count_ref, left_ref, right_ref, *refs):
    blocks, (out_ref, tiles, sums, sems) = refs[:-4], refs[-4:]
    n_x, n_z = out_ref.shape[:2]
    targets, tile, _ = sums.shape
    sec_dev = blocks[0].shape[0]
    pairs = left_ref.shape[0] * targets
    band = tile // (n_x * n_z)

    def fetch(b):
        return pltpu.make_async_copy(
            blocks[b], tiles.at[pl.ds(b * sec_dev, sec_dev)], sems.at[b]
        )

    for b in range(len(blocks)):
        fetch(b).start()
    sums[...] = jnp.zeros_like(sums)

    def step(g, ready):
        codes = [list_ref[g * GROUP + j] for j in range(GROUP)]
        origins = [lax.div(code, pairs) for code in codes]
        needed = lax.div(functools.reduce(jnp.maximum, origins), sec_dev) + 1
        for b in range(len(blocks)):
            pl.when(jnp.logical_and(ready <= b, b < needed))(fetch(b).wait)
        images = []
        for j in range(GROUP):
            pair = lax.rem(codes[j], pairs)
            term = lax.div(pair, targets)
            mixed = jnp.dot(
                left_ref[term], tiles[origins[j]], preferred_element_type=jnp.float32
            ).astype(jnp.bfloat16)
            image = jnp.dot(mixed, right_ref[term], preferred_element_type=jnp.float32)
            images.append((lax.rem(pair, targets), image * weight_ref[g * GROUP + j]))
        for target, image in images:
            sums[target] += image
        return jnp.maximum(ready, needed)

    ready = lax.fori_loop(0, lax.div(count_ref[0] + GROUP - 1, GROUP), step, 0)
    for b in range(len(blocks)):
        pl.when(ready <= b)(fetch(b).wait)
    for t in range(0, targets, 2):
        two = [sums[t + i].reshape(n_z, n_x, band, tile) for i in range(2)]
        rows = jnp.concatenate(two, axis=2).astype(out_ref.dtype)
        for x in range(n_x):
            out_ref[x, :, pl.ds(t * band, 2 * band), :] = rows[:, x]


def per_device(psi, left_ops, right_ops, coef, source, active, left_block, right_block):
    sec_dev, tile, _ = psi.shape
    term_dev = left_ops.shape[0]
    n_z, n_x, n_y, cores = (lax.axis_size(name) for name in NAMES)
    n_ops = n_z * n_x
    targets = 2 * sec_dev
    pairs = term_dev * targets
    band = tile // n_ops
    sources = len(PLACES) * 2 * sec_dev
    ops_index = lax.axis_index("z") * n_x + lax.axis_index("x")
    core = lax.axis_index("core").astype(jnp.int32)
    ring = lax.axis_index("y").astype(jnp.int32)
    smem = pl.BlockSpec(memory_space=pltpu.SMEM)
    vmem = pl.BlockSpec(memory_space=pltpu.VMEM)
    anywhere = pl.BlockSpec(memory_space=pl.ANY)

    def from_y(value, away):
        pairs = [(((y + a) % n_y) * 2 + c, y * 2 + c) for y in range(n_y) for c, a in ((0, away), (1, -away))]
        return lax.ppermute(value, ("y", "core"), pairs)

    def from_core(value):
        return lax.ppermute(value, "core", [(0, 1), (1, 0)])

    code = jnp.where(active != 0, source, -1)
    code, psi_out = lax.optimization_barrier((code, psi))
    codes = jnp.concatenate([code, from_y(code, n_y // 2)], axis=1)
    near = [from_y(psi_out, 1), from_y(psi_out, -1)]
    their_psi = from_core(psi_out)
    pair_list, weights, count, left_near, right_near = pl.pallas_call(
        plan_kernel,
        out_shape=(
            jax.ShapeDtypeStruct((pairs + GROUP,), jnp.int32),
            jax.ShapeDtypeStruct((pairs + GROUP,), jnp.float32),
            jax.ShapeDtypeStruct((1,), jnp.int32),
            jax.ShapeDtypeStruct(left_ops.shape, left_ops.dtype),
            jax.ShapeDtypeStruct(right_ops.shape, right_ops.dtype),
        ),
        in_specs=[smem] * 2 + [anywhere] * 2,
        out_specs=(smem,) * 3 + (vmem,) * 2,
        scratch_shapes=[
            pltpu.SMEM((sources + 1,), jnp.int32),
            pltpu.SemaphoreType.DMA((2,)),
        ],
        compiler_params=pltpu.CompilerParams(vmem_limit_bytes=56 * 2**20),
        name="plan",
    )(places_of(codes, sec_dev, core, ring).reshape(pairs), coef, left_ops, right_ops)

    count, near = lax.optimization_barrier((count, near))
    mine = [psi, *near, from_y(near[0], 1)]
    theirs = [their_psi] + [from_core(block) for block in mine[1:]]
    blocks = [None] * (2 * len(PLACES))
    for (_, other, own), my_block, their_block in zip(PLACES, mine, theirs):
        blocks[own], blocks[other] = my_block, their_block

    partial_sum = pl.pallas_call(
        terms_kernel,
        out_shape=jax.ShapeDtypeStruct((n_x, n_z, targets * band, tile), jnp.bfloat16),
        in_specs=[smem] * 3 + [vmem] * 2 + [anywhere] * len(blocks),
        out_specs=vmem,
        scratch_shapes=[
            pltpu.VMEM((sources, tile, tile), psi.dtype),
            pltpu.VMEM((targets, tile, tile), jnp.float32),
            pltpu.SemaphoreType.DMA((len(blocks),)),
        ],
        compiler_params=pltpu.CompilerParams(vmem_limit_bytes=24 * 2**20),
        cost_estimate=pl.CostEstimate(
            flops=pairs * tile**3, bytes_accessed=10 * 2**20, transcendentals=0
        ),
        name="terms",
    )(pair_list, weights, count, left_near, right_near, *blocks)

    local_rows = lax.dynamic_slice_in_dim(psi, ops_index * band, band, 1)
    block_rows = lax.dynamic_slice_in_dim(left_block, ops_index * band, band, 1)
    local_part = jnp.einsum("tij,tjl->til", block_rows, psi, preferred_element_type=jnp.float32)
    local_part = local_part + jnp.einsum(
        "tij,tjl->til", local_rows, right_block, preferred_element_type=jnp.float32
    )

    bands = lax.all_to_all(partial_sum, "x", 0, 0, tiled=True)
    bands = pl.pallas_call(
        add_kernel,
        out_shape=jax.ShapeDtypeStruct(bands.shape[1:], bands.dtype),
        in_specs=[vmem],
        out_specs=vmem,
        name="add",
    )(bands)
    bands = lax.all_to_all(bands, "z", 0, 0, tiled=True)
    summed = jnp.sum(bands.astype(jnp.float32), axis=0).reshape(2, sec_dev, band, tile)
    return local_part + summed[0] + from_y(summed[1], n_y // 2)


def solution(mesh):
    full = Mesh(mesh.devices.reshape(AXES), NAMES)
    ops, sec = ("z", "x"), ("y", "core")
    in_specs = (
        P(sec, None, None),
        P(ops, None, None),
        P(ops, None, None),
        P(ops),
        P(ops, sec),
        P(ops, sec),
        P(sec, None, None),
        P(sec, None, None),
    )
    return jax.shard_map(
        per_device, mesh=full, in_specs=in_specs, out_specs=P(sec, ops, None), check_vma=False
    )
```

```python
import functools

import jax
import jax.numpy as jnp
from jax import lax
from jax.experimental import pallas as pl
from jax.experimental.pallas import tpu as pltpu
from jax.sharding import Mesh, PartitionSpec as P

AXES = (8, 4, 2, 4, 2)
NAMES = ("z", "x", "half", "y", "core")
GROUP = 4

PLACES = ((0, 1, 0), (1, 4, 2), (-1, 5, 3), (2, 7, 6))
EARLY = 2


def places_of(codes, sec_dev, core, ring, length):
    source_core = (codes // sec_dev) % 2
    away = (codes // (2 * sec_dev) - ring) * jnp.where(source_core == 0, 1, -1)
    block = jnp.full_like(codes, -1)
    for far, other, own in PLACES:
        here = (away - far) % length == 0
        block = jnp.where(here, jnp.where(source_core == core, own, other), block)
    held = jnp.logical_and(codes >= 0, block >= 0)
    return jnp.where(held, block * sec_dev + codes % sec_dev, 2 * len(PLACES) * sec_dev)


def sorted_pairs(places):
    pairs = places.shape[0]
    pair = jnp.arange(pairs, dtype=jnp.int32)
    keys = places * pairs + pair
    rank = jnp.sum((keys[None, :] < keys[:, None]).astype(jnp.int32), axis=1)
    return jnp.sum(jnp.where(rank[None, :] == pair[:, None], keys[None, :], 0), axis=1)


def add_pairs(first, last, first_place, list_ref, coef_ref, left_ref, right_ref, blocks, tiles, sems, sums):
    targets = sums.shape[0]
    pairs = list_ref.shape[0]
    sec_dev = blocks[0].shape[0]

    def fetch(b):
        return pltpu.make_async_copy(
            blocks[b], tiles.at[pl.ds(b * sec_dev, sec_dev)], sems.at[b]
        )

    def step(g, ready):
        work = []
        for j in range(GROUP):
            at = first + g * GROUP + j
            valid = at < last
            code = list_ref[jnp.minimum(at, pairs - 1)]
            code = jnp.where(valid, code, pairs * first_place)
            pair = lax.rem(code, pairs)
            term = lax.div(pair, targets)
            weight = jnp.where(valid, coef_ref[term], 0.0)
            work.append((lax.div(code, pairs) - first_place, term, lax.rem(pair, targets), weight))
        needed = lax.div(functools.reduce(jnp.maximum, [w[0] for w in work]), sec_dev) + 1
        for b in range(len(blocks)):
            pl.when(jnp.logical_and(ready <= b, b < needed))(fetch(b).wait)
        images = []
        for place, term, target, weight in work:
            mixed = jnp.dot(
                left_ref[term], tiles[place], preferred_element_type=jnp.float32
            ).astype(jnp.bfloat16)
            image = jnp.dot(mixed, right_ref[term], preferred_element_type=jnp.float32)
            images.append((target, image * weight))
        for target, image in images:
            sums[target] += image
        return jnp.maximum(ready, needed)

    ready = lax.fori_loop(0, lax.div(last - first + GROUP - 1, GROUP), step, 0)
    for b in range(len(blocks)):
        pl.when(ready <= b)(fetch(b).wait)


def start_fetches(blocks, tiles, sems):
    sec_dev = blocks[0].shape[0]
    for b, block in enumerate(blocks):
        pltpu.make_async_copy(block, tiles.at[pl.ds(b * sec_dev, sec_dev)], sems.at[b]).start()


def early_kernel(list_ref, count_ref, coef_ref, left_hbm, right_hbm, *refs):
    blocks, (sums, left_ref, right_ref, tiles, sems, op_sems) = refs[:-6], refs[-6:]
    copies = [
        pltpu.make_async_copy(left_hbm, left_ref, op_sems.at[0]),
        pltpu.make_async_copy(right_hbm, right_ref, op_sems.at[1]),
    ]
    for copy in copies:
        copy.start()
    start_fetches(blocks, tiles, sems)
    sums[...] = jnp.zeros_like(sums)
    for copy in copies:
        copy.wait()
    add_pairs(0, count_ref[0], 0, list_ref, coef_ref, left_ref, right_ref, blocks, tiles, sems, sums)


def terms_kernel(list_ref, count_ref, coef_ref, left_ref, right_ref, early_ref, *refs):
    blocks, (out_ref, tiles, sums, sems) = refs[:-4], refs[-4:]
    n_x, n_z = out_ref.shape[:2]
    targets, tile, _ = sums.shape
    band = tile // (n_x * n_z)
    start_fetches(blocks, tiles, sems)
    sums[...] = early_ref[...]
    add_pairs(
        count_ref[0], count_ref[1], EARLY * blocks[0].shape[0],
        list_ref, coef_ref, left_ref, right_ref, blocks, tiles, sems, sums,
    )
    for t in range(0, targets, 2):
        two = [sums[t + i].reshape(n_z, n_x, band, tile) for i in range(2)]
        rows = jnp.concatenate(two, axis=2).astype(out_ref.dtype)
        for x in range(n_x):
            out_ref[x, :, pl.ds(t * band, 2 * band), :] = rows[:, x]


def add_kernel(parts_ref, out_ref):
    def add(i, carry):
        total = parts_ref[0, i].astype(jnp.float32)
        for part in range(1, parts_ref.shape[0]):
            total += parts_ref[part, i].astype(jnp.float32)
        out_ref[i] = total.astype(out_ref.dtype)
        return carry

    lax.fori_loop(0, out_ref.shape[0], add, 0)


def per_device(psi, left_ops, right_ops, coef, source, active, left_block, right_block):
    sec_dev, tile, _ = psi.shape
    term_dev = left_ops.shape[0]
    n_z, n_x, halves, half_y, cores = (lax.axis_size(name) for name in NAMES)
    n_ops, n_y = n_z * n_x, halves * half_y
    targets = halves * sec_dev
    pairs = term_dev * targets
    band = tile // n_ops
    ops_index = lax.axis_index("z") * n_x + lax.axis_index("x")
    core, half = lax.axis_index("core"), lax.axis_index("half")
    ring = half * half_y + lax.axis_index("y")
    smem = pl.BlockSpec(memory_space=pltpu.SMEM)
    vmem = pl.BlockSpec(memory_space=pltpu.VMEM)
    anywhere = pl.BlockSpec(memory_space=pl.ANY)

    def from_y(value, away):
        route = [(((y + a) % n_y) * 2 + c, y * 2 + c) for y in range(n_y) for c, a in ((0, away), (1, -away))]
        return lax.ppermute(value, ("half", "y", "core"), route)

    def from_core(value):
        return lax.ppermute(value, "core", [(0, 1), (1, 0)])

    far = from_y(psi, 2)
    near = [from_y(psi, 1), from_y(psi, -1)]
    their_psi = from_core(psi)

    code = jnp.where(active != 0, source, -1)
    other = from_y(code, n_y // 2)
    codes = jnp.concatenate(
        [jnp.where(half == 0, code, other), jnp.where(half == 0, other, code)], axis=1
    )
    places = places_of(codes, sec_dev, core, ring, n_y).reshape(pairs)
    pair_list = sorted_pairs(places)
    limits = jnp.array([EARLY, 2 * len(PLACES)], jnp.int32) * sec_dev
    counts = jnp.sum((places[None, :] < limits[:, None]).astype(jnp.int32), axis=1)

    early, left_near, right_near = pl.pallas_call(
        early_kernel,
        out_shape=(
            jax.ShapeDtypeStruct((targets, tile, tile), jnp.float32),
            jax.ShapeDtypeStruct(left_ops.shape, left_ops.dtype),
            jax.ShapeDtypeStruct(right_ops.shape, right_ops.dtype),
        ),
        in_specs=[smem] * 3 + [anywhere] * (2 + EARLY),
        out_specs=(vmem,) * 3,
        scratch_shapes=[
            pltpu.VMEM((EARLY * sec_dev, tile, tile), psi.dtype),
            pltpu.SemaphoreType.DMA((EARLY,)),
            pltpu.SemaphoreType.DMA((2,)),
        ],
        compiler_params=pltpu.CompilerParams(vmem_limit_bytes=16 * 2**20),
        name="early",
    )(pair_list, counts, coef, left_ops, right_ops, psi, their_psi)

    early, near = lax.optimization_barrier((early, near))
    mine = [psi, *near, far]
    theirs = [their_psi] + [from_core(block) for block in mine[1:]]
    blocks = [None] * (2 * len(PLACES))
    for (_, other, own), my_block, their_block in zip(PLACES, mine, theirs):
        blocks[own], blocks[other] = my_block, their_block
    blocks = blocks[EARLY:]

    partial_sum = pl.pallas_call(
        terms_kernel,
        out_shape=jax.ShapeDtypeStruct((n_x, n_z, targets * band, tile), jnp.bfloat16),
        in_specs=[smem] * 3 + [vmem] * 3 + [anywhere] * len(blocks),
        out_specs=vmem,
        scratch_shapes=[
            pltpu.VMEM((len(blocks) * sec_dev, tile, tile), psi.dtype),
            pltpu.VMEM((targets, tile, tile), jnp.float32),
            pltpu.SemaphoreType.DMA((len(blocks),)),
        ],
        compiler_params=pltpu.CompilerParams(vmem_limit_bytes=24 * 2**20),
        name="terms",
    )(pair_list, counts, coef, left_near, right_near, early, *blocks)

    local_rows = lax.dynamic_slice_in_dim(psi, ops_index * band, band, 1)
    block_rows = lax.dynamic_slice_in_dim(left_block, ops_index * band, band, 1)
    local_part = jnp.einsum("tij,tjl->til", block_rows, psi, preferred_element_type=jnp.float32)
    local_part = local_part + jnp.einsum(
        "tij,tjl->til", local_rows, right_block, preferred_element_type=jnp.float32
    )

    bands = lax.all_to_all(partial_sum, "x", 0, 0, tiled=True)
    bands = pl.pallas_call(
        add_kernel,
        out_shape=jax.ShapeDtypeStruct(bands.shape[1:], bands.dtype),
        in_specs=[vmem],
        out_specs=vmem,
        name="add",
    )(bands)
    bands = bands.reshape(n_z * halves, sec_dev * band, tile)
    bands = lax.all_to_all(bands, ("z", "half"), 0, 0, tiled=True)
    summed = jnp.sum(bands.astype(jnp.float32), axis=0).reshape(sec_dev, band, tile)
    return local_part + summed


def solution(mesh):
    full = Mesh(mesh.devices.reshape(AXES), NAMES)
    ops, sec = ("z", "x"), ("half", "y", "core")
    in_specs = (
        P(sec, None, None),
        P(ops, None, None),
        P(ops, None, None),
        P(ops),
        P(ops, sec),
        P(ops, sec),
        P(sec, None, None),
        P(sec, None, None),
    )
    return jax.shard_map(
        per_device, mesh=full, in_specs=in_specs, out_specs=P(sec, ops, None), check_vma=False
    )
```

```python
import functools

import jax
import jax.numpy as jnp
from jax import lax
from jax.experimental import pallas as pl
from jax.experimental.pallas import tpu as pltpu
from jax.sharding import Mesh, PartitionSpec as P

AXES = (8, 4, 2, 4, 2)
NAMES = ("z", "x", "half", "y", "core")
GROUP = 4

PLACES = ((0, 1, 0), (1, 4, 2), (-1, 5, 3), (2, 7, 6))


def places_of(codes, sec_dev, core, ring, length):
    source_core = (codes // sec_dev) % 2
    away = (codes // (2 * sec_dev) - ring) * jnp.where(source_core == 0, 1, -1)
    block = jnp.full_like(codes, -1)
    for far, other, own in PLACES:
        here = (away - far) % length == 0
        block = jnp.where(here, jnp.where(source_core == core, own, other), block)
    held = jnp.logical_and(codes >= 0, block >= 0)
    return jnp.where(held, block * sec_dev + codes % sec_dev, 2 * len(PLACES) * sec_dev)


def sorted_pairs(places):
    pairs = places.shape[0]
    pair = jnp.arange(pairs, dtype=jnp.int32)
    keys = places * pairs + pair
    rank = jnp.sum((keys[None, :] < keys[:, None]).astype(jnp.int32), axis=1)
    return jnp.sum(jnp.where(rank[None, :] == pair[:, None], keys[None, :], 0), axis=1)


def add_pairs(last, list_ref, coef_ref, left_ref, right_ref, blocks, tiles, sems, sums):
    targets = sums.shape[0]
    pairs = list_ref.shape[0]
    sec_dev = blocks[0].shape[0]

    def fetch(b):
        return pltpu.make_async_copy(
            blocks[b], tiles.at[pl.ds(b * sec_dev, sec_dev)], sems.at[b]
        )

    def step(g, ready):
        work = []
        for j in range(GROUP):
            at = g * GROUP + j
            valid = at < last
            code = list_ref[jnp.minimum(at, pairs - 1)]
            code = jnp.where(valid, code, 0)
            pair = lax.rem(code, pairs)
            term = lax.div(pair, targets)
            weight = jnp.where(valid, coef_ref[term], 0.0)
            work.append((lax.div(code, pairs), term, lax.rem(pair, targets), weight))
        needed = lax.div(functools.reduce(jnp.maximum, [w[0] for w in work]), sec_dev) + 1
        for b in range(len(blocks)):
            pl.when(jnp.logical_and(ready <= b, b < needed))(fetch(b).wait)
        images = []
        for place, term, target, weight in work:
            mixed = jnp.dot(
                left_ref[term], tiles[place], preferred_element_type=jnp.float32
            ).astype(jnp.bfloat16)
            image = jnp.dot(mixed, right_ref[term], preferred_element_type=jnp.float32)
            images.append((target, image * weight))
        for target, image in images:
            sums[target] += image
        return jnp.maximum(ready, needed)

    ready = lax.fori_loop(0, lax.div(last + GROUP - 1, GROUP), step, 0)
    for b in range(len(blocks)):
        pl.when(ready <= b)(fetch(b).wait)


def start_fetches(blocks, tiles, sems):
    sec_dev = blocks[0].shape[0]
    for b, block in enumerate(blocks):
        pltpu.make_async_copy(block, tiles.at[pl.ds(b * sec_dev, sec_dev)], sems.at[b]).start()


def hold_kernel(left_hbm, right_hbm, left_ref, right_ref, sems):
    copies = [
        pltpu.make_async_copy(left_hbm, left_ref, sems.at[0]),
        pltpu.make_async_copy(right_hbm, right_ref, sems.at[1]),
    ]
    for copy in copies:
        copy.start()
    for copy in copies:
        copy.wait()


def terms_kernel(list_ref, count_ref, coef_ref, left_ref, right_ref, *refs):
    blocks, (out_ref, tiles, sums, sems) = refs[:-4], refs[-4:]
    n_x, n_z = out_ref.shape[:2]
    targets, tile, _ = sums.shape
    band = tile // (n_x * n_z)
    start_fetches(blocks, tiles, sems)
    sums[...] = jnp.zeros_like(sums)
    add_pairs(count_ref[0], list_ref, coef_ref, left_ref, right_ref, blocks, tiles, sems, sums)
    for t in range(0, targets, 2):
        two = [sums[t + i].reshape(n_z, n_x, band, tile) for i in range(2)]
        rows = jnp.concatenate(two, axis=2).astype(out_ref.dtype)
        for x in range(n_x):
            out_ref[x, :, pl.ds(t * band, 2 * band), :] = rows[:, x]


def per_device(psi, left_ops, right_ops, coef, source, active, left_block, right_block):
    sec_dev, tile, _ = psi.shape
    term_dev = left_ops.shape[0]
    n_z, n_x, halves, half_y, cores = (lax.axis_size(name) for name in NAMES)
    n_ops, n_y = n_z * n_x, halves * half_y
    targets = halves * sec_dev
    pairs = term_dev * targets
    band = tile // n_ops
    ops_index = lax.axis_index("z") * n_x + lax.axis_index("x")
    core, half = lax.axis_index("core"), lax.axis_index("half")
    ring = half * half_y + lax.axis_index("y")
    smem = pl.BlockSpec(memory_space=pltpu.SMEM)
    vmem = pl.BlockSpec(memory_space=pltpu.VMEM)
    anywhere = pl.BlockSpec(memory_space=pl.ANY)

    def from_y(value, away):
        route = [(((y + a) % n_y) * 2 + c, y * 2 + c) for y in range(n_y) for c, a in ((0, away), (1, -away))]
        return lax.ppermute(value, ("half", "y", "core"), route)

    def from_core(value):
        return lax.ppermute(value, "core", [(0, 1), (1, 0)])

    near = [from_y(psi, 1), from_y(psi, -1)]
    far = from_y(psi, 2)
    their_psi = from_core(psi)
    code = jnp.where(active != 0, source, -1)
    other = from_y(code, n_y // 2)
    held = pl.pallas_call(
        hold_kernel,
        out_shape=(
            jax.ShapeDtypeStruct(left_ops.shape, left_ops.dtype),
            jax.ShapeDtypeStruct(right_ops.shape, right_ops.dtype),
        ),
        in_specs=[anywhere] * 2,
        out_specs=(vmem,) * 2,
        scratch_shapes=[pltpu.SemaphoreType.DMA((2,))],
        compiler_params=pltpu.CompilerParams(vmem_limit_bytes=16 * 2**20),
        name="hold",
    )(left_ops, right_ops)

    local_rows = lax.dynamic_slice_in_dim(psi, ops_index * band, band, 1)
    block_rows = lax.dynamic_slice_in_dim(left_block, ops_index * band, band, 1)
    local_part = jnp.einsum("tij,tjl->til", block_rows, psi, preferred_element_type=jnp.float32)
    local_part = local_part + jnp.einsum(
        "tij,tjl->til", local_rows, right_block, preferred_element_type=jnp.float32
    )

    near, held, local_part = lax.optimization_barrier((near, held, local_part))
    theirs = [their_psi] + [from_core(block) for block in near]
    far, other, theirs = lax.optimization_barrier((far, other, theirs))
    theirs.append(from_core(far))
    blocks = [None] * (2 * len(PLACES))
    for (_, other_place, own), my_block, their_block in zip(PLACES, [psi, *near, far], theirs):
        blocks[own], blocks[other_place] = my_block, their_block

    codes = jnp.concatenate(
        [jnp.where(half == 0, code, other), jnp.where(half == 0, other, code)], axis=1
    )
    places = places_of(codes, sec_dev, core, ring, n_y).reshape(pairs)
    count = jnp.sum((places < len(blocks) * sec_dev).astype(jnp.int32)).reshape(1)

    partial_sum = pl.pallas_call(
        terms_kernel,
        out_shape=jax.ShapeDtypeStruct((n_x, n_z, targets * band, tile), jnp.bfloat16),
        in_specs=[smem] * 3 + [vmem] * 2 + [anywhere] * len(blocks),
        out_specs=vmem,
        scratch_shapes=[
            pltpu.VMEM((len(blocks) * sec_dev, tile, tile), psi.dtype),
            pltpu.VMEM((targets, tile, tile), jnp.float32),
            pltpu.SemaphoreType.DMA((len(blocks),)),
        ],
        compiler_params=pltpu.CompilerParams(vmem_limit_bytes=24 * 2**20),
        name="terms",
    )(sorted_pairs(places), count, coef, *held, *blocks)

    bands = lax.all_to_all(partial_sum, "x", 0, 0, tiled=True)
    bands = lax.optimization_barrier(jnp.sum(bands.astype(jnp.float32), axis=0))
    bands = bands.astype(partial_sum.dtype)
    bands = bands.reshape(n_z * halves, sec_dev * band, tile)
    bands = lax.all_to_all(bands, ("z", "half"), 0, 0, tiled=True)
    summed = jnp.sum(bands.astype(jnp.float32), axis=0).reshape(sec_dev, band, tile)
    return local_part + summed


def solution(mesh):
    full = Mesh(mesh.devices.reshape(AXES), NAMES)
    ops, sec = ("z", "x"), ("half", "y", "core")
    in_specs = (
        P(sec, None, None),
        P(ops, None, None),
        P(ops, None, None),
        P(ops),
        P(ops, sec),
        P(ops, sec),
        P(sec, None, None),
        P(sec, None, None),
    )
    return jax.shard_map(
        per_device, mesh=full, in_specs=in_specs, out_specs=P(sec, ops, None), check_vma=False
    )
```

```python
import functools

import jax
import jax.numpy as jnp
from jax import lax
from jax.experimental import pallas as pl
from jax.experimental.pallas import tpu as pltpu
from jax.sharding import Mesh, PartitionSpec as P

AXES = (8, 4, 2, 4, 2)
NAMES = ("z", "x", "half", "y", "core")
GROUP = 4

PLACES = ((0, 1, 0), (1, 4, 2), (-1, 5, 3), (2, 7, 6))


def places_of(codes, sec_dev, core, ring, length):
    source_core = (codes // sec_dev) % 2
    away = (codes // (2 * sec_dev) - ring) * jnp.where(source_core == 0, 1, -1)
    block = jnp.full_like(codes, -1)
    for far, other, own in PLACES:
        here = (away - far) % length == 0
        block = jnp.where(here, jnp.where(source_core == core, own, other), block)
    held = jnp.logical_and(codes >= 0, block >= 0)
    return jnp.where(held, block * sec_dev + codes % sec_dev, 2 * len(PLACES) * sec_dev)


def sorted_pairs(places):
    pairs = places.shape[0]
    pair = jnp.arange(pairs, dtype=jnp.int32)
    keys = places * pairs + pair
    rank = jnp.sum((keys[None, :] < keys[:, None]).astype(jnp.int32), axis=1)
    return jnp.sum(jnp.where(rank[None, :] == pair[:, None], keys[None, :], 0), axis=1)


def terms_kernel(list_ref, coef_ref, left_hbm, right_hbm, *refs):
    blocks, (out_ref, left_ref, right_ref, tiles, sums, sems) = refs[:-6], refs[-6:]
    n_x, n_z = out_ref.shape[:2]
    targets, tile, _ = sums.shape
    band = tile // (n_x * n_z)
    pairs = list_ref.shape[0]
    sec_dev = blocks[0].shape[0]
    end = pairs * sec_dev * len(blocks)

    def fetch(b):
        return pltpu.make_async_copy(
            blocks[b], tiles.at[pl.ds(b * sec_dev, sec_dev)], sems.at[b]
        )

    operators = [
        pltpu.make_async_copy(left_hbm, left_ref, sems.at[len(blocks)]),
        pltpu.make_async_copy(right_hbm, right_ref, sems.at[len(blocks) + 1]),
    ]
    for copy in operators:
        copy.start()
    for b in range(len(blocks)):
        fetch(b).start()
    sums[...] = jnp.zeros_like(sums)
    for copy in operators:
        copy.wait()

    def more(state):
        at, _ = state
        return jnp.logical_and(at < pairs, list_ref[jnp.minimum(at, pairs - 1)] < end)

    def step(state):
        at, ready = state
        work = []
        for j in range(GROUP):
            code = list_ref[at + j]
            valid = code < end
            code = jnp.where(valid, code, 0)
            pair = lax.rem(code, pairs)
            term = lax.div(pair, targets)
            weight = jnp.where(valid, coef_ref[term], 0.0)
            work.append((lax.div(code, pairs), term, lax.rem(pair, targets), weight))
        needed = lax.div(functools.reduce(jnp.maximum, [w[0] for w in work]), sec_dev) + 1
        for b in range(len(blocks)):
            pl.when(jnp.logical_and(ready <= b, b < needed))(fetch(b).wait)
        images = []
        for place, term, target, weight in work:
            mixed = jnp.dot(
                left_ref[term], tiles[place], preferred_element_type=jnp.float32
            ).astype(jnp.bfloat16)
            image = jnp.dot(mixed, right_ref[term], preferred_element_type=jnp.float32)
            images.append((target, image * weight))
        for target, image in images:
            sums[target] += image
        return at + GROUP, jnp.maximum(ready, needed)

    _, ready = lax.while_loop(more, step, (0, 0))
    for b in range(len(blocks)):
        pl.when(ready <= b)(fetch(b).wait)
    for t in range(0, targets, 2):
        two = [sums[t + i].reshape(n_z, n_x, band, tile) for i in range(2)]
        rows = jnp.concatenate(two, axis=2).astype(out_ref.dtype)
        for x in range(n_x):
            out_ref[x, :, pl.ds(t * band, 2 * band), :] = rows[:, x]


def per_device(psi, left_ops, right_ops, coef, source, active, left_block, right_block):
    sec_dev, tile, _ = psi.shape
    term_dev = left_ops.shape[0]
    n_z, n_x, halves, half_y, cores = (lax.axis_size(name) for name in NAMES)
    n_ops, n_y = n_z * n_x, halves * half_y
    targets = halves * sec_dev
    pairs = term_dev * targets
    band = tile // n_ops
    ops_index = lax.axis_index("z") * n_x + lax.axis_index("x")
    core, half = lax.axis_index("core"), lax.axis_index("half")
    ring = half * half_y + lax.axis_index("y")
    smem = pl.BlockSpec(memory_space=pltpu.SMEM)
    vmem = pl.BlockSpec(memory_space=pltpu.VMEM)
    anywhere = pl.BlockSpec(memory_space=pl.ANY)

    def from_y(value, away):
        route = [(((y + a) % n_y) * 2 + c, y * 2 + c) for y in range(n_y) for c, a in ((0, away), (1, -away))]
        return lax.ppermute(value, ("half", "y", "core"), route)

    def from_core(value):
        return lax.ppermute(value, "core", [(0, 1), (1, 0)])

    near = [from_y(psi, 1), from_y(psi, -1)]
    their_psi = from_core(psi)
    code = jnp.where(active != 0, source, -1)
    other = from_y(code, n_y // 2)
    local_rows = lax.dynamic_slice_in_dim(psi, ops_index * band, band, 1)
    block_rows = lax.dynamic_slice_in_dim(left_block, ops_index * band, band, 1)
    local_part = jnp.einsum("tij,tjl->til", block_rows, psi, preferred_element_type=jnp.float32)
    local_part = local_part + jnp.einsum(
        "tij,tjl->til", local_rows, right_block, preferred_element_type=jnp.float32
    )

    near, other, local_part = lax.optimization_barrier((near[::-1], other, local_part))
    near = near[::-1]
    far = from_y(near[0], 1)

    codes = jnp.concatenate(
        [jnp.where(half == 0, code, other), jnp.where(half == 0, other, code)], axis=1
    )
    pair_list = sorted_pairs(places_of(codes, sec_dev, core, ring, n_y).reshape(pairs))

    theirs = [their_psi] + [from_core(block) for block in near]
    theirs, far, pair_list = lax.optimization_barrier((theirs[::-1], far, pair_list))
    theirs = theirs[::-1]
    theirs.append(from_core(far))
    blocks = [None] * (2 * len(PLACES))
    for (_, other_place, own), my_block, their_block in zip(PLACES, [psi, *near, far], theirs):
        blocks[own], blocks[other_place] = my_block, their_block

    partial_sum = pl.pallas_call(
        terms_kernel,
        out_shape=jax.ShapeDtypeStruct((n_x, n_z, targets * band, tile), jnp.bfloat16),
        in_specs=[smem] * 2 + [anywhere] * (2 + len(blocks)),
        out_specs=vmem,
        scratch_shapes=[
            pltpu.VMEM(left_ops.shape, left_ops.dtype),
            pltpu.VMEM(right_ops.shape, right_ops.dtype),
            pltpu.VMEM((len(blocks) * sec_dev, tile, tile), psi.dtype),
            pltpu.VMEM((targets, tile, tile), jnp.float32),
            pltpu.SemaphoreType.DMA((len(blocks) + 2,)),
        ],
        compiler_params=pltpu.CompilerParams(vmem_limit_bytes=48 * 2**20),
        name="terms",
    )(pair_list, coef, left_ops, right_ops, *blocks)

    bands = lax.all_to_all(partial_sum, "x", 0, 0, tiled=True)
    bands = lax.optimization_barrier(jnp.sum(bands.astype(jnp.float32), axis=0))
    bands = bands.astype(partial_sum.dtype)
    bands = bands.reshape(n_z * halves, sec_dev * band, tile)
    bands = lax.all_to_all(bands, ("z", "half"), 0, 0, tiled=True)
    summed = jnp.sum(bands.astype(jnp.float32), axis=0).reshape(sec_dev, band, tile)
    return local_part + summed


def solution(mesh):
    full = Mesh(mesh.devices.reshape(AXES), NAMES)
    ops, sec = ("z", "x"), ("half", "y", "core")
    in_specs = (
        P(sec, None, None),
        P(ops, None, None),
        P(ops, None, None),
        P(ops),
        P(ops, sec),
        P(ops, sec),
        P(sec, None, None),
        P(sec, None, None),
    )
    return jax.shard_map(
        per_device, mesh=full, in_specs=in_specs, out_specs=P(sec, ops, None), check_vma=False
    )
```

```python
import functools

import jax
import jax.numpy as jnp
from jax import lax
from jax.experimental import pallas as pl
from jax.experimental.pallas import tpu as pltpu
from jax.sharding import Mesh, PartitionSpec as P

AXES = (8, 4, 2, 4, 2)
NAMES = ("z", "x", "half", "y", "core")
GROUP = 4

PLACES = ((0, 1, 0), (1, 4, 2), (-1, 5, 3), (2, 7, 6))


def places_of(codes, sec_dev, core, ring, length):
    source_core = (codes // sec_dev) % 2
    away = (codes // (2 * sec_dev) - ring) * jnp.where(source_core == 0, 1, -1)
    block = jnp.full_like(codes, -1)
    for far, other, own in PLACES:
        here = (away - far) % length == 0
        block = jnp.where(here, jnp.where(source_core == core, own, other), block)
    held = jnp.logical_and(codes >= 0, block >= 0)
    return jnp.where(held, block * sec_dev + codes % sec_dev, 2 * len(PLACES) * sec_dev)


def sorted_pairs(places, weights):
    pairs = places.shape[0]
    pair = jnp.arange(pairs, dtype=jnp.int32)
    keys = places * pairs + pair
    rank = jnp.sum((keys[None, :] < keys[:, None]).astype(jnp.int32), axis=1)
    here = rank[None, :] == pair[:, None]
    listed = jnp.sum(jnp.where(here, keys[None, :], 0), axis=1)
    return listed, jnp.sum(jnp.where(here, weights[None, :], 0.0), axis=1)


def terms_kernel(list_ref, weight_ref, left_hbm, right_hbm, *refs):
    blocks, (out_ref, left_ref, right_ref, tiles, sums, sems) = refs[:-6], refs[-6:]
    n_x, n_z = out_ref.shape[:2]
    targets, tile, _ = sums.shape
    band = tile // (n_x * n_z)
    pairs = list_ref.shape[0]
    sec_dev = blocks[0].shape[0]
    end = pairs * sec_dev * len(blocks)

    def fetch(b):
        return pltpu.make_async_copy(
            blocks[b], tiles.at[pl.ds(b * sec_dev, sec_dev)], sems.at[b]
        )

    operators = [
        pltpu.make_async_copy(left_hbm, left_ref, sems.at[len(blocks)]),
        pltpu.make_async_copy(right_hbm, right_ref, sems.at[len(blocks) + 1]),
    ]
    for copy in operators:
        copy.start()
    for b in range(len(blocks)):
        fetch(b).start()
    sums[...] = jnp.zeros_like(sums)
    for copy in operators:
        copy.wait()

    def more(state):
        at, _ = state
        return jnp.logical_and(at < pairs, list_ref[jnp.minimum(at, pairs - 1)] < end)

    def step(state):
        at, ready = state
        work = []
        for j in range(GROUP):
            code = list_ref[at + j]
            valid = code < end
            code = jnp.where(valid, code, 0)
            pair = lax.rem(code, pairs)
            term = lax.div(pair, targets)
            weight = jnp.where(valid, weight_ref[at + j], 0.0)
            work.append((lax.div(code, pairs), term, lax.rem(pair, targets), weight))
        needed = lax.div(functools.reduce(jnp.maximum, [w[0] for w in work]), sec_dev) + 1
        for b in range(len(blocks)):
            pl.when(jnp.logical_and(ready <= b, b < needed))(fetch(b).wait)
        images = []
        for place, term, target, weight in work:
            mixed = jnp.dot(
                left_ref[term], tiles[place], preferred_element_type=jnp.float32
            ).astype(jnp.bfloat16)
            image = jnp.dot(mixed, right_ref[term], preferred_element_type=jnp.float32)
            images.append((target, image * weight))
        for target, image in images:
            sums[target] += image
        return at + GROUP, jnp.maximum(ready, needed)

    _, ready = lax.while_loop(more, step, (0, 0))
    for b in range(len(blocks)):
        pl.when(ready <= b)(fetch(b).wait)
    for t in range(0, targets, 2):
        two = [sums[t + i].reshape(n_z, n_x, band, tile) for i in range(2)]
        rows = jnp.concatenate(two, axis=2).astype(out_ref.dtype)
        for x in range(n_x):
            out_ref[x, :, pl.ds(t * band, 2 * band), :] = rows[:, x]


def per_device(psi, left_ops, right_ops, coef, source, active, left_block, right_block):
    sec_dev, tile, _ = psi.shape
    term_dev = left_ops.shape[0]
    n_z, n_x, halves, half_y, cores = (lax.axis_size(name) for name in NAMES)
    n_ops, n_y = n_z * n_x, halves * half_y
    targets = halves * sec_dev
    pairs = term_dev * targets
    band = tile // n_ops
    ops_index = lax.axis_index("z") * n_x + lax.axis_index("x")
    core, half = lax.axis_index("core"), lax.axis_index("half")
    ring = half * half_y + lax.axis_index("y")
    smem = pl.BlockSpec(memory_space=pltpu.SMEM)
    vmem = pl.BlockSpec(memory_space=pltpu.VMEM)
    anywhere = pl.BlockSpec(memory_space=pl.ANY)

    def from_y(value, away):
        route = [(((y + a) % n_y) * 2 + c, y * 2 + c) for y in range(n_y) for c, a in ((0, away), (1, -away))]
        return lax.ppermute(value, ("half", "y", "core"), route)

    def from_core(value):
        return lax.ppermute(value, "core", [(0, 1), (1, 0)])

    near = [from_y(psi, 1), from_y(psi, -1)]
    code = jnp.where(active != 0, source, -1)
    other = from_y(code, n_y // 2)
    local_rows = lax.dynamic_slice_in_dim(psi, ops_index * band, band, 1)
    block_rows = lax.dynamic_slice_in_dim(left_block, ops_index * band, band, 1)
    local_part = jnp.einsum("tij,tjl->til", block_rows, psi, preferred_element_type=jnp.float32)
    local_part = local_part + jnp.einsum(
        "tij,tjl->til", local_rows, right_block, preferred_element_type=jnp.float32
    )

    near, other, local_part, psi = lax.optimization_barrier((near[::-1], other, local_part, psi))
    near = near[::-1]
    far = from_y(near[0], 1)

    codes = jnp.concatenate(
        [jnp.where(half == 0, code, other), jnp.where(half == 0, other, code)], axis=1
    )
    places = places_of(codes, sec_dev, core, ring, n_y).reshape(pairs)
    listed = sorted_pairs(places, jnp.repeat(coef, targets))

    theirs = [from_core(block) for block in [psi, *near]]
    theirs, far, listed = lax.optimization_barrier((theirs[::-1], far, listed))
    theirs = theirs[::-1]
    theirs.append(from_core(far))
    blocks = [None] * (2 * len(PLACES))
    for (_, other_place, own), my_block, their_block in zip(PLACES, [psi, *near, far], theirs):
        blocks[own], blocks[other_place] = my_block, their_block

    partial_sum = pl.pallas_call(
        terms_kernel,
        out_shape=jax.ShapeDtypeStruct((n_x, n_z, targets * band, tile), jnp.bfloat16),
        in_specs=[smem] * 2 + [anywhere] * (2 + len(blocks)),
        out_specs=vmem,
        scratch_shapes=[
            pltpu.VMEM(left_ops.shape, left_ops.dtype),
            pltpu.VMEM(right_ops.shape, right_ops.dtype),
            pltpu.VMEM((len(blocks) * sec_dev, tile, tile), psi.dtype),
            pltpu.VMEM((targets, tile, tile), jnp.float32),
            pltpu.SemaphoreType.DMA((len(blocks) + 2,)),
        ],
        compiler_params=pltpu.CompilerParams(vmem_limit_bytes=48 * 2**20),
        name="terms",
    )(*listed, left_ops, right_ops, *blocks)

    bands = lax.all_to_all(partial_sum, "x", 0, 0, tiled=True)
    bands = lax.optimization_barrier(jnp.sum(bands.astype(jnp.float32), axis=0))
    bands = bands.astype(partial_sum.dtype)
    bands = bands.reshape(n_z * halves, sec_dev * band, tile)
    bands = lax.all_to_all(bands, ("z", "half"), 0, 0, tiled=True)
    summed = jnp.sum(bands.astype(jnp.float32), axis=0).reshape(sec_dev, band, tile)
    return local_part + summed


def solution(mesh):
    full = Mesh(mesh.devices.reshape(AXES), NAMES)
    ops, sec = ("z", "x"), ("half", "y", "core")
    in_specs = (
        P(sec, None, None),
        P(ops, None, None),
        P(ops, None, None),
        P(ops),
        P(ops, sec),
        P(ops, sec),
        P(sec, None, None),
        P(sec, None, None),
    )
    return jax.shard_map(
        per_device, mesh=full, in_specs=in_specs, out_specs=P(sec, ops, None), check_vma=False
    )
```

```python
import functools

import jax
import jax.numpy as jnp
from jax import lax
from jax.experimental import pallas as pl
from jax.experimental.pallas import tpu as pltpu
from jax.sharding import Mesh, PartitionSpec as P

AXES = (8, 4, 2, 4, 2)
NAMES = ("z", "x", "half", "y", "core")
GROUP = 4

PLACES = ((0, 1, 0), (1, 4, 2), (-1, 5, 3), (2, 7, 6))


def places_of(codes, sec_dev, core, ring, length):
    source_core = (codes // sec_dev) % 2
    away = (codes // (2 * sec_dev) - ring) * jnp.where(source_core == 0, 1, -1)
    block = jnp.full_like(codes, -1)
    for far, other, own in PLACES:
        here = (away - far) % length == 0
        block = jnp.where(here, jnp.where(source_core == core, own, other), block)
    held = jnp.logical_and(codes >= 0, block >= 0)
    return jnp.where(held, block * sec_dev + codes % sec_dev, 2 * len(PLACES) * sec_dev)


def sorted_pairs(places, weights):
    pairs = places.shape[0]
    pair = jnp.arange(pairs, dtype=jnp.int32)
    keys = places * pairs + pair
    rank = jnp.sum((keys[None, :] < keys[:, None]).astype(jnp.int32), axis=1)
    here = rank[None, :] == pair[:, None]
    listed = jnp.sum(jnp.where(here, keys[None, :], 0), axis=1)
    return listed, jnp.sum(jnp.where(here, weights[None, :], 0.0), axis=1)


def terms_kernel(list_ref, weight_ref, left_hbm, right_hbm, *refs):
    blocks, (out_ref, left_ref, right_ref, tiles, sums, sems) = refs[:-6], refs[-6:]
    n_x, n_z = out_ref.shape[:2]
    targets, tile, _ = sums.shape
    band = tile // (n_x * n_z)
    pairs = list_ref.shape[0]
    sec_dev = blocks[0].shape[0]
    end = pairs * sec_dev * len(blocks)

    def fetch(b):
        return pltpu.make_async_copy(
            blocks[b], tiles.at[pl.ds(b * sec_dev, sec_dev)], sems.at[b]
        )

    operators = [
        pltpu.make_async_copy(left_hbm, left_ref, sems.at[len(blocks)]),
        pltpu.make_async_copy(right_hbm, right_ref, sems.at[len(blocks) + 1]),
    ]
    for copy in operators:
        copy.start()
    for b in range(len(blocks)):
        fetch(b).start()
    sums[...] = jnp.zeros_like(sums)
    for copy in operators:
        copy.wait()

    def more(state):
        at, _ = state
        return jnp.logical_and(at < pairs, list_ref[jnp.minimum(at, pairs - 1)] < end)

    def step(state):
        at, ready = state
        work = []
        for j in range(GROUP):
            code = list_ref[at + j]
            valid = code < end
            code = jnp.where(valid, code, 0)
            pair = lax.rem(code, pairs)
            term = lax.div(pair, targets)
            weight = jnp.where(valid, weight_ref[at + j], 0.0)
            work.append((lax.div(code, pairs), term, lax.rem(pair, targets), weight))
        needed = lax.div(functools.reduce(jnp.maximum, [w[0] for w in work]), sec_dev) + 1
        for b in range(len(blocks)):
            pl.when(jnp.logical_and(ready <= b, b < needed))(fetch(b).wait)
        images = []
        for place, term, target, weight in work:
            mixed = jnp.dot(
                left_ref[term], tiles[place], preferred_element_type=jnp.float32
            ).astype(jnp.bfloat16)
            image = jnp.dot(mixed, right_ref[term], preferred_element_type=jnp.float32)
            images.append((target, image * weight))
        for target, image in images:
            sums[target] += image
        return at + GROUP, jnp.maximum(ready, needed)

    _, ready = lax.while_loop(more, step, (0, 0))
    for b in range(len(blocks)):
        pl.when(ready <= b)(fetch(b).wait)
    for t in range(0, targets, 2):
        two = [sums[t + i].reshape(n_z, n_x, band, tile) for i in range(2)]
        rows = jnp.concatenate(two, axis=2).astype(out_ref.dtype)
        for x in range(n_x):
            out_ref[x, :, pl.ds(t * band, 2 * band), :] = rows[:, x]


def per_device(psi, left_ops, right_ops, coef, source, active, left_block, right_block):
    sec_dev, tile, _ = psi.shape
    term_dev = left_ops.shape[0]
    n_z, n_x, halves, half_y, cores = (lax.axis_size(name) for name in NAMES)
    n_ops, n_y = n_z * n_x, halves * half_y
    targets = halves * sec_dev
    pairs = term_dev * targets
    band = tile // n_ops
    ops_index = lax.axis_index("z") * n_x + lax.axis_index("x")
    core, half = lax.axis_index("core"), lax.axis_index("half")
    ring = half * half_y + lax.axis_index("y")
    smem = pl.BlockSpec(memory_space=pltpu.SMEM)
    vmem = pl.BlockSpec(memory_space=pltpu.VMEM)
    anywhere = pl.BlockSpec(memory_space=pl.ANY)

    def from_y(value, away):
        route = [(((y + a) % n_y) * 2 + c, y * 2 + c) for y in range(n_y) for c, a in ((0, away), (1, -away))]
        return lax.ppermute(value, ("half", "y", "core"), route)

    def from_core(value):
        return lax.ppermute(value, "core", [(0, 1), (1, 0)])

    first = from_y(psi, 1)
    code = jnp.where(active != 0, source, -1)
    other = from_y(code, n_y // 2)
    local_rows = lax.dynamic_slice_in_dim(psi, ops_index * band, band, 1)
    block_rows = lax.dynamic_slice_in_dim(left_block, ops_index * band, band, 1)
    local_part = jnp.einsum("tij,tjl->til", block_rows, psi, preferred_element_type=jnp.float32)
    local_part = local_part + jnp.einsum(
        "tij,tjl->til", local_rows, right_block, preferred_element_type=jnp.float32
    )

    first, other, local_part, psi = lax.optimization_barrier((first, other, local_part, psi))
    far = from_y(first, 1)
    near = [first, from_y(psi, -1)]

    codes = jnp.concatenate(
        [jnp.where(half == 0, code, other), jnp.where(half == 0, other, code)], axis=1
    )
    places = places_of(codes, sec_dev, core, ring, n_y).reshape(pairs)
    listed = sorted_pairs(places, jnp.repeat(coef, targets))

    theirs = [from_core(block) for block in [psi, *near]]
    theirs, far, listed = lax.optimization_barrier((theirs[::-1], far, listed))
    theirs = theirs[::-1]
    theirs.append(from_core(far))
    blocks = [None] * (2 * len(PLACES))
    for (_, other_place, own), my_block, their_block in zip(PLACES, [psi, *near, far], theirs):
        blocks[own], blocks[other_place] = my_block, their_block

    partial_sum = pl.pallas_call(
        terms_kernel,
        out_shape=jax.ShapeDtypeStruct((n_x, n_z, targets * band, tile), jnp.bfloat16),
        in_specs=[smem] * 2 + [anywhere] * (2 + len(blocks)),
        out_specs=vmem,
        scratch_shapes=[
            pltpu.VMEM(left_ops.shape, left_ops.dtype),
            pltpu.VMEM(right_ops.shape, right_ops.dtype),
            pltpu.VMEM((len(blocks) * sec_dev, tile, tile), psi.dtype),
            pltpu.VMEM((targets, tile, tile), jnp.float32),
            pltpu.SemaphoreType.DMA((len(blocks) + 2,)),
        ],
        compiler_params=pltpu.CompilerParams(vmem_limit_bytes=48 * 2**20),
        name="terms",
    )(*listed, left_ops, right_ops, *blocks)

    bands = lax.all_to_all(partial_sum, "x", 0, 0, tiled=True)
    bands = lax.optimization_barrier(jnp.sum(bands.astype(jnp.float32), axis=0))
    bands = bands.astype(partial_sum.dtype)
    bands = bands.reshape(n_z * halves, sec_dev * band, tile)
    bands = lax.all_to_all(bands, ("z", "half"), 0, 0, tiled=True)
    summed = jnp.sum(bands.astype(jnp.float32), axis=0).reshape(sec_dev, band, tile)
    return local_part + summed


def solution(mesh):
    full = Mesh(mesh.devices.reshape(AXES), NAMES)
    ops, sec = ("z", "x"), ("half", "y", "core")
    in_specs = (
        P(sec, None, None),
        P(ops, None, None),
        P(ops, None, None),
        P(ops),
        P(ops, sec),
        P(ops, sec),
        P(sec, None, None),
        P(sec, None, None),
    )
    return jax.shard_map(
        per_device, mesh=full, in_specs=in_specs, out_specs=P(sec, ops, None), check_vma=False
    )
```

```python
import functools

import jax
import jax.numpy as jnp
from jax import lax
from jax.experimental import pallas as pl
from jax.experimental.pallas import tpu as pltpu
from jax.sharding import Mesh, PartitionSpec as P

AXES = (8, 4, 2, 4, 2)
NAMES = ("z", "x", "half", "y", "core")
GROUP = 4
PARTS = 2

PLACES = ((0, 1, 0), (1, 4, 2), (-1, 5, 3), (2, 7, 6))


def places_of(codes, sec_dev, core, ring, length):
    source_core = (codes // sec_dev) % 2
    away = (codes // (2 * sec_dev) - ring) * jnp.where(source_core == 0, 1, -1)
    block = jnp.full_like(codes, -1)
    for far, other, own in PLACES:
        here = (away - far) % length == 0
        block = jnp.where(here, jnp.where(source_core == core, own, other), block)
    held = jnp.logical_and(codes >= 0, block >= 0)
    return jnp.where(held, block * sec_dev + codes % sec_dev, 2 * len(PLACES) * sec_dev)


def sorted_pairs(places, weights):
    pairs = places.shape[0]
    pair = jnp.arange(pairs, dtype=jnp.int32)
    keys = places * pairs + pair
    rank = jnp.sum((keys[None, :] < keys[:, None]).astype(jnp.int32), axis=1)
    here = rank[None, :] == pair[:, None]
    listed = jnp.sum(jnp.where(here, keys[None, :], 0), axis=1)
    return listed, jnp.sum(jnp.where(here, weights[None, :], 0.0), axis=1)


def terms_kernel(list_ref, weight_ref, left_hbm, right_hbm, *refs):
    blocks, (out_ref, left_ref, right_ref, tiles, sums, sems) = refs[:-6], refs[-6:]
    n_x, n_z = out_ref.shape[:2]
    targets, tile, _ = sums.shape
    band = tile // (n_x * n_z)
    pairs = list_ref.shape[0]
    sec_dev = blocks[0].shape[0]
    end = pairs * sec_dev * len(blocks)

    def fetch(b):
        return pltpu.make_async_copy(
            blocks[b], tiles.at[pl.ds(b * sec_dev, sec_dev)], sems.at[b]
        )

    operators = [
        pltpu.make_async_copy(left_hbm, left_ref, sems.at[len(blocks)]),
        pltpu.make_async_copy(right_hbm, right_ref, sems.at[len(blocks) + 1]),
    ]
    for copy in operators:
        copy.start()
    for b in range(len(blocks)):
        fetch(b).start()
    sums[...] = jnp.zeros_like(sums)
    for copy in operators:
        copy.wait()

    def more(state):
        at, _ = state
        return jnp.logical_and(at < pairs, list_ref[jnp.minimum(at, pairs - 1)] < end)

    def step(state):
        at, ready = state
        work = []
        for j in range(GROUP):
            code = list_ref[at + j]
            valid = code < end
            code = jnp.where(valid, code, 0)
            pair = lax.rem(code, pairs)
            term = lax.div(pair, targets)
            weight = jnp.where(valid, weight_ref[at + j], 0.0)
            work.append((lax.div(code, pairs), term, lax.rem(pair, targets), weight))
        needed = lax.div(functools.reduce(jnp.maximum, [w[0] for w in work]), sec_dev) + 1
        for b in range(len(blocks)):
            pl.when(jnp.logical_and(ready <= b, b < needed))(fetch(b).wait)
        images = []
        for place, term, target, weight in work:
            mixed = jnp.dot(
                left_ref[term], tiles[place], preferred_element_type=jnp.float32
            ).astype(jnp.bfloat16)
            image = jnp.dot(mixed, right_ref[term], preferred_element_type=jnp.float32)
            images.append((target, image * weight))
        for target, image in images:
            sums[target] += image
        return at + GROUP, jnp.maximum(ready, needed)

    _, ready = lax.while_loop(more, step, (0, 0))
    for b in range(len(blocks)):
        pl.when(ready <= b)(fetch(b).wait)
    for t in range(0, targets, 2):
        two = [sums[t + i].reshape(n_z, n_x, band, tile) for i in range(2)]
        rows = jnp.concatenate(two, axis=2).astype(out_ref.dtype)
        for x in range(n_x):
            out_ref[x, :, pl.ds(t * band, 2 * band), :] = rows[:, x]


def per_device(psi, left_ops, right_ops, coef, source, active, left_block, right_block):
    sec_dev, tile, _ = psi.shape
    term_dev = left_ops.shape[0]
    n_z, n_x, halves, half_y, cores = (lax.axis_size(name) for name in NAMES)
    n_ops, n_y = n_z * n_x, halves * half_y
    part = sec_dev // PARTS
    band = tile // n_ops
    ops_index = lax.axis_index("z") * n_x + lax.axis_index("x")
    core, half = lax.axis_index("core"), lax.axis_index("half")
    ring = half * half_y + lax.axis_index("y")
    smem = pl.BlockSpec(memory_space=pltpu.SMEM)
    vmem = pl.BlockSpec(memory_space=pltpu.VMEM)
    anywhere = pl.BlockSpec(memory_space=pl.ANY)

    def from_y(value, away):
        route = [(((y + a) % n_y) * 2 + c, y * 2 + c) for y in range(n_y) for c, a in ((0, away), (1, -away))]
        return lax.ppermute(value, ("half", "y", "core"), route)

    def from_core(value):
        return lax.ppermute(value, "core", [(0, 1), (1, 0)])

    near = [from_y(psi, 1), from_y(psi, -1)]
    code = jnp.where(active != 0, source, -1)
    other = from_y(code, n_y // 2)
    local_rows = lax.dynamic_slice_in_dim(psi, ops_index * band, band, 1)
    block_rows = lax.dynamic_slice_in_dim(left_block, ops_index * band, band, 1)
    local_part = jnp.einsum("tij,tjl->til", block_rows, psi, preferred_element_type=jnp.float32)
    local_part = local_part + jnp.einsum(
        "tij,tjl->til", local_rows, right_block, preferred_element_type=jnp.float32
    )

    near, other, local_part, psi = lax.optimization_barrier((near[::-1], other, local_part, psi))
    near = near[::-1]
    far = from_y(near[0], 1)

    codes = jnp.concatenate(
        [jnp.where(half == 0, code, other), jnp.where(half == 0, other, code)], axis=1
    )
    places = places_of(codes, sec_dev, core, ring, n_y).reshape(term_dev, halves, PARTS, part)
    weights = jnp.repeat(coef, halves * part)
    listed = [sorted_pairs(places[:, :, p].reshape(-1), weights) for p in range(PARTS)]

    theirs = [from_core(block) for block in [psi, *near]]
    theirs, far, listed = lax.optimization_barrier((theirs[::-1], far, listed))
    theirs = theirs[::-1]
    theirs.append(from_core(far))
    blocks = [None] * (2 * len(PLACES))
    for (_, other_place, own), my_block, their_block in zip(PLACES, [psi, *near, far], theirs):
        blocks[own], blocks[other_place] = my_block, their_block

    def sums_of(part_list):
        return pl.pallas_call(
            terms_kernel,
            out_shape=jax.ShapeDtypeStruct((n_x, n_z, halves * part * band, tile), jnp.bfloat16),
            in_specs=[smem] * 2 + [anywhere] * (2 + len(blocks)),
            out_specs=vmem,
            scratch_shapes=[
                pltpu.VMEM(left_ops.shape, left_ops.dtype),
                pltpu.VMEM(right_ops.shape, right_ops.dtype),
                pltpu.VMEM((len(blocks) * sec_dev, tile, tile), psi.dtype),
                pltpu.VMEM((halves * part, tile, tile), jnp.float32),
                pltpu.SemaphoreType.DMA((len(blocks) + 2,)),
            ],
            compiler_params=pltpu.CompilerParams(vmem_limit_bytes=48 * 2**20),
            name="terms",
        )(*part_list, left_ops, right_ops, *blocks)

    sums = [sums_of(part_list) for part_list in listed]
    along_x = [lax.all_to_all(part_sums, "x", 0, 0, tiled=True) for part_sums in sums]
    along_x[0], _ = lax.optimization_barrier((along_x[0], sums[-1]))
    done = []
    for bands in along_x:
        bands = lax.optimization_barrier(jnp.sum(bands.astype(jnp.float32), axis=0))
        bands = bands.astype(jnp.bfloat16).reshape(n_z * halves, part * band, tile)
        bands = lax.all_to_all(bands, ("z", "half"), 0, 0, tiled=True)
        done.append(jnp.sum(bands.astype(jnp.float32), axis=0).reshape(part, band, tile))
    return local_part + jnp.concatenate(done, axis=0)


def solution(mesh):
    full = Mesh(mesh.devices.reshape(AXES), NAMES)
    ops, sec = ("z", "x"), ("half", "y", "core")
    in_specs = (
        P(sec, None, None),
        P(ops, None, None),
        P(ops, None, None),
        P(ops),
        P(ops, sec),
        P(ops, sec),
        P(sec, None, None),
        P(sec, None, None),
    )
    return jax.shard_map(
        per_device, mesh=full, in_specs=in_specs, out_specs=P(sec, ops, None), check_vma=False
    )
```

```python
import functools

import jax
import jax.numpy as jnp
from jax import lax
from jax.experimental import pallas as pl
from jax.experimental.pallas import tpu as pltpu
from jax.sharding import Mesh, PartitionSpec as P

AXES = (8, 4, 2, 4, 2)
NAMES = ("z", "x", "half", "y", "core")
GROUP = 4

PLACES = ((0, 1, 0), (1, 4, 2), (-1, 5, 3), (2, 7, 6))


def places_of(codes, sec_dev, core, ring, length):
    source_core = (codes // sec_dev) % 2
    away = (codes // (2 * sec_dev) - ring) * jnp.where(source_core == 0, 1, -1)
    block = jnp.full_like(codes, -1)
    for far, other, own in PLACES:
        here = (away - far) % length == 0
        block = jnp.where(here, jnp.where(source_core == core, own, other), block)
    held = jnp.logical_and(codes >= 0, block >= 0)
    return jnp.where(held, block * sec_dev + codes % sec_dev, 2 * len(PLACES) * sec_dev)


def sorted_pairs(places, weights):
    pairs = places.shape[0]
    pair = jnp.arange(pairs, dtype=jnp.int32)
    keys = places * pairs + pair
    rank = jnp.sum((keys[None, :] < keys[:, None]).astype(jnp.int32), axis=1)
    here = rank[None, :] == pair[:, None]
    listed = jnp.sum(jnp.where(here, keys[None, :], 0), axis=1)
    return listed, jnp.sum(jnp.where(here, weights[None, :], 0.0), axis=1)


def terms_kernel(list_ref, weight_ref, left_hbm, right_hbm, *refs):
    blocks, (out_ref, left_ref, right_ref, tiles, sums, sems) = refs[:-6], refs[-6:]
    n_x, n_z = out_ref.shape[:2]
    targets, tile, _ = sums.shape
    band = tile // (n_x * n_z)
    pairs = list_ref.shape[0]
    sec_dev = blocks[0].shape[0]
    end = pairs * sec_dev * len(blocks)

    def fetch(b):
        return pltpu.make_async_copy(
            blocks[b], tiles.at[pl.ds(b * sec_dev, sec_dev)], sems.at[b]
        )

    operators = [
        pltpu.make_async_copy(left_hbm, left_ref, sems.at[len(blocks)]),
        pltpu.make_async_copy(right_hbm, right_ref, sems.at[len(blocks) + 1]),
    ]
    for copy in operators:
        copy.start()
    for b in range(len(blocks)):
        fetch(b).start()
    sums[...] = jnp.zeros_like(sums)
    for copy in operators:
        copy.wait()

    def more(state):
        at, _ = state
        return jnp.logical_and(at < pairs, list_ref[jnp.minimum(at, pairs - 1)] < end)

    def step(state):
        at, ready = state
        work = []
        for j in range(GROUP):
            code = list_ref[at + j]
            valid = code < end
            code = jnp.where(valid, code, 0)
            pair = lax.rem(code, pairs)
            term = lax.div(pair, targets)
            weight = jnp.where(valid, weight_ref[at + j], 0.0)
            work.append((lax.div(code, pairs), term, lax.rem(pair, targets), weight))
        needed = lax.div(functools.reduce(jnp.maximum, [w[0] for w in work]), sec_dev) + 1
        for b in range(len(blocks)):
            pl.when(jnp.logical_and(ready <= b, b < needed))(fetch(b).wait)
        images = []
        for place, term, target, weight in work:
            mixed = jnp.dot(
                left_ref[term], tiles[place], preferred_element_type=jnp.float32
            ).astype(jnp.bfloat16)
            image = jnp.dot(mixed, right_ref[term], preferred_element_type=jnp.float32)
            images.append((target, image * weight))
        for target, image in images:
            sums[target] += image
        return at + GROUP, jnp.maximum(ready, needed)

    _, ready = lax.while_loop(more, step, (0, 0))
    for b in range(len(blocks)):
        pl.when(ready <= b)(fetch(b).wait)
    for t in range(0, targets, 2):
        two = [sums[t + i].reshape(n_z, n_x, band, tile) for i in range(2)]
        rows = jnp.concatenate(two, axis=2).astype(out_ref.dtype)
        for x in range(n_x):
            out_ref[x, :, pl.ds(t * band, 2 * band), :] = rows[:, x]


def per_device(psi, left_ops, right_ops, coef, source, active, left_block, right_block):
    sec_dev, tile, _ = psi.shape
    term_dev = left_ops.shape[0]
    n_z, n_x, halves, half_y, cores = (lax.axis_size(name) for name in NAMES)
    n_ops, n_y = n_z * n_x, halves * half_y
    targets = halves * sec_dev
    pairs = term_dev * targets
    band = tile // n_ops
    ops_index = lax.axis_index("z") * n_x + lax.axis_index("x")
    core, half = lax.axis_index("core"), lax.axis_index("half")
    ring = half * half_y + lax.axis_index("y")
    smem = pl.BlockSpec(memory_space=pltpu.SMEM)
    vmem = pl.BlockSpec(memory_space=pltpu.VMEM)
    anywhere = pl.BlockSpec(memory_space=pl.ANY)

    def from_y(value, away):
        route = [(((y + a) % n_y) * 2 + c, y * 2 + c) for y in range(n_y) for c, a in ((0, away), (1, -away))]
        return lax.ppermute(value, ("half", "y", "core"), route)

    def from_core(value):
        return lax.ppermute(value, "core", [(0, 1), (1, 0)])

    near = [from_y(psi, 1), from_y(psi, -1)]
    far = from_y(psi, 2)
    code = jnp.where(active != 0, source, -1)
    other = from_y(code, n_y // 2)
    local_rows = lax.dynamic_slice_in_dim(psi, ops_index * band, band, 1)
    block_rows = lax.dynamic_slice_in_dim(left_block, ops_index * band, band, 1)
    local_part = jnp.einsum("tij,tjl->til", block_rows, psi, preferred_element_type=jnp.float32)
    local_part = local_part + jnp.einsum(
        "tij,tjl->til", local_rows, right_block, preferred_element_type=jnp.float32
    )

    near, other, local_part, psi = lax.optimization_barrier((near[::-1], other, local_part, psi))
    near = near[::-1]

    codes = jnp.concatenate(
        [jnp.where(half == 0, code, other), jnp.where(half == 0, other, code)], axis=1
    )
    places = places_of(codes, sec_dev, core, ring, n_y).reshape(pairs)
    listed = sorted_pairs(places, jnp.repeat(coef, targets))

    theirs = [from_core(block) for block in [psi, *near]]
    theirs, far, listed = lax.optimization_barrier((theirs[::-1], far, listed))
    theirs = theirs[::-1]
    theirs.append(from_core(far))
    blocks = [None] * (2 * len(PLACES))
    for (_, other_place, own), my_block, their_block in zip(PLACES, [psi, *near, far], theirs):
        blocks[own], blocks[other_place] = my_block, their_block

    partial_sum = pl.pallas_call(
        terms_kernel,
        out_shape=jax.ShapeDtypeStruct((n_x, n_z, targets * band, tile), jnp.bfloat16),
        in_specs=[smem] * 2 + [anywhere] * (2 + len(blocks)),
        out_specs=vmem,
        scratch_shapes=[
            pltpu.VMEM(left_ops.shape, left_ops.dtype),
            pltpu.VMEM(right_ops.shape, right_ops.dtype),
            pltpu.VMEM((len(blocks) * sec_dev, tile, tile), psi.dtype),
            pltpu.VMEM((targets, tile, tile), jnp.float32),
            pltpu.SemaphoreType.DMA((len(blocks) + 2,)),
        ],
        compiler_params=pltpu.CompilerParams(vmem_limit_bytes=48 * 2**20),
        name="terms",
    )(*listed, left_ops, right_ops, *blocks)

    bands = lax.all_to_all(partial_sum, "x", 0, 0, tiled=True)
    bands = lax.optimization_barrier(jnp.sum(bands.astype(jnp.float32), axis=0))
    bands = bands.astype(partial_sum.dtype)
    bands = bands.reshape(n_z * halves, sec_dev * band, tile)
    bands = lax.all_to_all(bands, ("z", "half"), 0, 0, tiled=True)
    summed = jnp.sum(bands.astype(jnp.float32), axis=0).reshape(sec_dev, band, tile)
    return local_part + summed


def solution(mesh):
    full = Mesh(mesh.devices.reshape(AXES), NAMES)
    ops, sec = ("z", "x"), ("half", "y", "core")
    in_specs = (
        P(sec, None, None),
        P(ops, None, None),
        P(ops, None, None),
        P(ops),
        P(ops, sec),
        P(ops, sec),
        P(sec, None, None),
        P(sec, None, None),
    )
    return jax.shard_map(
        per_device, mesh=full, in_specs=in_specs, out_specs=P(sec, ops, None), check_vma=False
    )
```

```python
import functools

import jax
import jax.numpy as jnp
from jax import lax
from jax.experimental import pallas as pl
from jax.experimental.pallas import tpu as pltpu
from jax.sharding import Mesh, PartitionSpec as P

AXES = (8, 4, 2, 4, 2)
NAMES = ("z", "x", "half", "y", "core")
GROUP = 4

PLACES = ((0, 1, 0), (1, 4, 2), (-1, 5, 3), (2, 7, 6))


def places_of(codes, sec_dev, core, ring, length):
    source_core = (codes // sec_dev) % 2
    away = (codes // (2 * sec_dev) - ring) * jnp.where(source_core == 0, 1, -1)
    block = jnp.full_like(codes, -1)
    for far, other, own in PLACES:
        here = (away - far) % length == 0
        block = jnp.where(here, jnp.where(source_core == core, own, other), block)
    held = jnp.logical_and(codes >= 0, block >= 0)
    return jnp.where(held, block * sec_dev + codes % sec_dev, 2 * len(PLACES) * sec_dev)


def sorted_pairs(places, weights):
    pairs = places.shape[0]
    pair = jnp.arange(pairs, dtype=jnp.int32)
    keys = places * pairs + pair
    rank = jnp.sum((keys[None, :] < keys[:, None]).astype(jnp.int32), axis=1)
    here = rank[None, :] == pair[:, None]
    listed = jnp.sum(jnp.where(here, keys[None, :], 0), axis=1)
    return listed, jnp.sum(jnp.where(here, weights[None, :], 0.0), axis=1)


def keep_kernel(block, kept_ref, sem):
    copy = pltpu.make_async_copy(block, kept_ref, sem)
    copy.start()
    copy.wait()


def terms_kernel(list_ref, weight_ref, left_hbm, right_hbm, *refs):
    blocks, (out_ref, left_ref, right_ref, tiles, sums, sems) = refs[:-6], refs[-6:]
    n_x, n_z = out_ref.shape[:2]
    targets, tile, _ = sums.shape
    band = tile // (n_x * n_z)
    pairs = list_ref.shape[0]
    sec_dev = blocks[0].shape[0]
    end = pairs * sec_dev * len(blocks)

    def fetch(b):
        return pltpu.make_async_copy(
            blocks[b], tiles.at[pl.ds(b * sec_dev, sec_dev)], sems.at[b]
        )

    operators = [
        pltpu.make_async_copy(left_hbm, left_ref, sems.at[len(blocks)]),
        pltpu.make_async_copy(right_hbm, right_ref, sems.at[len(blocks) + 1]),
    ]
    for copy in operators:
        copy.start()
    for b in range(len(blocks)):
        fetch(b).start()
    sums[...] = jnp.zeros_like(sums)
    for copy in operators:
        copy.wait()

    def more(state):
        at, _ = state
        return jnp.logical_and(at < pairs, list_ref[jnp.minimum(at, pairs - 1)] < end)

    def step(state):
        at, ready = state
        work = []
        for j in range(GROUP):
            code = list_ref[at + j]
            valid = code < end
            code = jnp.where(valid, code, 0)
            pair = lax.rem(code, pairs)
            term = lax.div(pair, targets)
            weight = jnp.where(valid, weight_ref[at + j], 0.0)
            work.append((lax.div(code, pairs), term, lax.rem(pair, targets), weight))
        needed = lax.div(functools.reduce(jnp.maximum, [w[0] for w in work]), sec_dev) + 1
        for b in range(len(blocks)):
            pl.when(jnp.logical_and(ready <= b, b < needed))(fetch(b).wait)
        images = []
        for place, term, target, weight in work:
            mixed = jnp.dot(
                left_ref[term], tiles[place], preferred_element_type=jnp.float32
            ).astype(jnp.bfloat16)
            image = jnp.dot(mixed, right_ref[term], preferred_element_type=jnp.float32)
            images.append((target, image * weight))
        for target, image in images:
            sums[target] += image
        return at + GROUP, jnp.maximum(ready, needed)

    _, ready = lax.while_loop(more, step, (0, 0))
    for b in range(len(blocks)):
        pl.when(ready <= b)(fetch(b).wait)
    for t in range(0, targets, 2):
        two = [sums[t + i].reshape(n_z, n_x, band, tile) for i in range(2)]
        rows = jnp.concatenate(two, axis=2).astype(out_ref.dtype)
        for x in range(n_x):
            out_ref[x, :, pl.ds(t * band, 2 * band), :] = rows[:, x]


def per_device(psi, left_ops, right_ops, coef, source, active, left_block, right_block):
    sec_dev, tile, _ = psi.shape
    term_dev = left_ops.shape[0]
    n_z, n_x, halves, half_y, cores = (lax.axis_size(name) for name in NAMES)
    n_ops, n_y = n_z * n_x, halves * half_y
    targets = halves * sec_dev
    pairs = term_dev * targets
    band = tile // n_ops
    ops_index = lax.axis_index("z") * n_x + lax.axis_index("x")
    core, half = lax.axis_index("core"), lax.axis_index("half")
    ring = half * half_y + lax.axis_index("y")
    smem = pl.BlockSpec(memory_space=pltpu.SMEM)
    vmem = pl.BlockSpec(memory_space=pltpu.VMEM)
    anywhere = pl.BlockSpec(memory_space=pl.ANY)

    def from_y(value, away):
        route = [(((y + a) % n_y) * 2 + c, y * 2 + c) for y in range(n_y) for c, a in ((0, away), (1, -away))]
        return lax.ppermute(value, ("half", "y", "core"), route)

    def from_core(value):
        return lax.ppermute(value, "core", [(0, 1), (1, 0)])

    near = [from_y(psi, 1), from_y(psi, -1)]
    code = jnp.where(active != 0, source, -1)
    other = from_y(code, n_y // 2)
    local_rows = lax.dynamic_slice_in_dim(psi, ops_index * band, band, 1)
    block_rows = lax.dynamic_slice_in_dim(left_block, ops_index * band, band, 1)
    local_part = jnp.einsum("tij,tjl->til", block_rows, psi, preferred_element_type=jnp.float32)
    local_part = local_part + jnp.einsum(
        "tij,tjl->til", local_rows, right_block, preferred_element_type=jnp.float32
    )

    own = pl.pallas_call(
        keep_kernel,
        out_shape=jax.ShapeDtypeStruct(psi.shape, psi.dtype),
        in_specs=[anywhere],
        out_specs=vmem,
        scratch_shapes=[pltpu.SemaphoreType.DMA],
        compiler_params=pltpu.CompilerParams(vmem_limit_bytes=48 * 2**20),
        name="keep",
    )(psi)

    near, other, local_part, psi = lax.optimization_barrier((near[::-1], other, local_part, own))
    near = near[::-1]
    far = from_y(near[0], 1)

    codes = jnp.concatenate(
        [jnp.where(half == 0, code, other), jnp.where(half == 0, other, code)], axis=1
    )
    places = places_of(codes, sec_dev, core, ring, n_y).reshape(pairs)
    listed = sorted_pairs(places, jnp.repeat(coef, targets))

    theirs = [from_core(block) for block in [psi, *near]]
    theirs, far, listed = lax.optimization_barrier((theirs[::-1], far, listed))
    theirs = theirs[::-1]
    theirs.append(from_core(far))
    blocks = [None] * (2 * len(PLACES))
    for (_, other_place, own), my_block, their_block in zip(PLACES, [psi, *near, far], theirs):
        blocks[own], blocks[other_place] = my_block, their_block

    partial_sum = pl.pallas_call(
        terms_kernel,
        out_shape=jax.ShapeDtypeStruct((n_x, n_z, targets * band, tile), jnp.bfloat16),
        in_specs=[smem] * 2 + [anywhere] * (2 + len(blocks)),
        out_specs=vmem,
        scratch_shapes=[
            pltpu.VMEM(left_ops.shape, left_ops.dtype),
            pltpu.VMEM(right_ops.shape, right_ops.dtype),
            pltpu.VMEM((len(blocks) * sec_dev, tile, tile), psi.dtype),
            pltpu.VMEM((targets, tile, tile), jnp.float32),
            pltpu.SemaphoreType.DMA((len(blocks) + 2,)),
        ],
        compiler_params=pltpu.CompilerParams(vmem_limit_bytes=48 * 2**20),
        name="terms",
    )(*listed, left_ops, right_ops, *blocks)

    bands = lax.all_to_all(partial_sum, "x", 0, 0, tiled=True)
    bands = lax.optimization_barrier(jnp.sum(bands.astype(jnp.float32), axis=0))
    bands = bands.astype(partial_sum.dtype)
    bands = bands.reshape(n_z * halves, sec_dev * band, tile)
    bands = lax.all_to_all(bands, ("z", "half"), 0, 0, tiled=True)
    summed = jnp.sum(bands.astype(jnp.float32), axis=0).reshape(sec_dev, band, tile)
    return local_part + summed


def solution(mesh):
    full = Mesh(mesh.devices.reshape(AXES), NAMES)
    ops, sec = ("z", "x"), ("half", "y", "core")
    in_specs = (
        P(sec, None, None),
        P(ops, None, None),
        P(ops, None, None),
        P(ops),
        P(ops, sec),
        P(ops, sec),
        P(sec, None, None),
        P(sec, None, None),
    )
    return jax.shard_map(
        per_device, mesh=full, in_specs=in_specs, out_specs=P(sec, ops, None), check_vma=False
    )
```

```python
import functools

import jax
import jax.numpy as jnp
from jax import lax
from jax.experimental import pallas as pl
from jax.experimental.pallas import tpu as pltpu
from jax.sharding import Mesh, PartitionSpec as P

AXES = (8, 4, 2, 4, 2)
NAMES = ("z", "x", "half", "y", "core")
GROUP = 4

PLACES = ((0, 1, 0), (1, 4, 2), (-1, 5, 3), (2, 7, 6))


def places_of(codes, sec_dev, core, ring, length):
    source_core = (codes // sec_dev) % 2
    away = (codes // (2 * sec_dev) - ring) * jnp.where(source_core == 0, 1, -1)
    block = jnp.full_like(codes, -1)
    for far, other, own in PLACES:
        here = (away - far) % length == 0
        block = jnp.where(here, jnp.where(source_core == core, own, other), block)
    held = jnp.logical_and(codes >= 0, block >= 0)
    return jnp.where(held, block * sec_dev + codes % sec_dev, 2 * len(PLACES) * sec_dev)


def sorted_pairs(places, weights):
    pairs = places.shape[0]
    pair = jnp.arange(pairs, dtype=jnp.int32)
    keys = places * pairs + pair
    rank = jnp.sum((keys[None, :] < keys[:, None]).astype(jnp.int32), axis=1)
    here = rank[None, :] == pair[:, None]
    listed = jnp.sum(jnp.where(here, keys[None, :], 0), axis=1)
    return listed, jnp.sum(jnp.where(here, weights[None, :], 0.0), axis=1)


def keep_kernel(block, kept_ref, sem):
    copy = pltpu.make_async_copy(block, kept_ref, sem)
    copy.start()
    copy.wait()


def terms_kernel(list_ref, weight_ref, left_hbm, right_hbm, *refs):
    blocks, (out_ref, left_ref, right_ref, tiles, sums, sems) = refs[:-6], refs[-6:]
    n_x, n_z = out_ref.shape[:2]
    targets, tile, _ = sums.shape
    band = tile // (n_x * n_z)
    pairs = list_ref.shape[0]
    sec_dev = blocks[0].shape[0]
    end = pairs * sec_dev * len(blocks)

    def fetch(b):
        return pltpu.make_async_copy(
            blocks[b], tiles.at[pl.ds(b * sec_dev, sec_dev)], sems.at[b]
        )

    operators = [
        pltpu.make_async_copy(left_hbm, left_ref, sems.at[len(blocks)]),
        pltpu.make_async_copy(right_hbm, right_ref, sems.at[len(blocks) + 1]),
    ]
    for copy in operators:
        copy.start()
    for b in range(len(blocks)):
        fetch(b).start()
    sums[...] = jnp.zeros_like(sums)
    for copy in operators:
        copy.wait()

    def more(state):
        at, _ = state
        return jnp.logical_and(at < pairs, list_ref[jnp.minimum(at, pairs - 1)] < end)

    def step(state):
        at, ready = state
        work = []
        for j in range(GROUP):
            code = list_ref[at + j]
            valid = code < end
            code = jnp.where(valid, code, 0)
            pair = lax.rem(code, pairs)
            term = lax.div(pair, targets)
            weight = jnp.where(valid, weight_ref[at + j], 0.0)
            work.append((lax.div(code, pairs), term, lax.rem(pair, targets), weight))
        needed = lax.div(functools.reduce(jnp.maximum, [w[0] for w in work]), sec_dev) + 1
        for b in range(len(blocks)):
            pl.when(jnp.logical_and(ready <= b, b < needed))(fetch(b).wait)
        mixed = [
            jnp.dot(left_ref[term], tiles[place], preferred_element_type=jnp.float32)
            for place, term, _, _ in work
        ]
        for value, (_, term, target, weight) in zip(mixed, work):
            image = jnp.dot(
                value.astype(jnp.bfloat16), right_ref[term], preferred_element_type=jnp.float32
            )
            sums[target] += image * weight
        return at + GROUP, jnp.maximum(ready, needed)

    _, ready = lax.while_loop(more, step, (0, 0))
    for b in range(len(blocks)):
        pl.when(ready <= b)(fetch(b).wait)
    for t in range(0, targets, 2):
        two = [sums[t + i].reshape(n_z, n_x, band, tile) for i in range(2)]
        rows = jnp.concatenate(two, axis=2).astype(out_ref.dtype)
        for x in range(n_x):
            out_ref[x, :, pl.ds(t * band, 2 * band), :] = rows[:, x]


def per_device(psi, left_ops, right_ops, coef, source, active, left_block, right_block):
    sec_dev, tile, _ = psi.shape
    term_dev = left_ops.shape[0]
    n_z, n_x, halves, half_y, cores = (lax.axis_size(name) for name in NAMES)
    n_ops, n_y = n_z * n_x, halves * half_y
    targets = halves * sec_dev
    pairs = term_dev * targets
    band = tile // n_ops
    ops_index = lax.axis_index("z") * n_x + lax.axis_index("x")
    core, half = lax.axis_index("core"), lax.axis_index("half")
    ring = half * half_y + lax.axis_index("y")
    smem = pl.BlockSpec(memory_space=pltpu.SMEM)
    vmem = pl.BlockSpec(memory_space=pltpu.VMEM)
    anywhere = pl.BlockSpec(memory_space=pl.ANY)

    def from_y(value, away):
        route = [(((y + a) % n_y) * 2 + c, y * 2 + c) for y in range(n_y) for c, a in ((0, away), (1, -away))]
        return lax.ppermute(value, ("half", "y", "core"), route)

    def from_core(value):
        return lax.ppermute(value, "core", [(0, 1), (1, 0)])

    near = [from_y(psi, 1), from_y(psi, -1)]
    code = jnp.where(active != 0, source, -1)
    other = from_y(code, n_y // 2)
    local_rows = lax.dynamic_slice_in_dim(psi, ops_index * band, band, 1)
    block_rows = lax.dynamic_slice_in_dim(left_block, ops_index * band, band, 1)
    local_part = jnp.einsum("tij,tjl->til", block_rows, psi, preferred_element_type=jnp.float32)
    local_part = local_part + jnp.einsum(
        "tij,tjl->til", local_rows, right_block, preferred_element_type=jnp.float32
    )

    own = pl.pallas_call(
        keep_kernel,
        out_shape=jax.ShapeDtypeStruct(psi.shape, psi.dtype),
        in_specs=[anywhere],
        out_specs=vmem,
        scratch_shapes=[pltpu.SemaphoreType.DMA],
        compiler_params=pltpu.CompilerParams(vmem_limit_bytes=48 * 2**20),
        name="keep",
    )(psi)

    near, other, local_part, psi = lax.optimization_barrier((near[::-1], other, local_part, own))
    near = near[::-1]
    far = from_y(near[0], 1)

    codes = jnp.concatenate(
        [jnp.where(half == 0, code, other), jnp.where(half == 0, other, code)], axis=1
    )
    places = places_of(codes, sec_dev, core, ring, n_y).reshape(pairs)
    listed = sorted_pairs(places, jnp.repeat(coef, targets))

    theirs = [from_core(block) for block in [psi, *near]]
    theirs, far, listed = lax.optimization_barrier((theirs[::-1], far, listed))
    theirs = theirs[::-1]
    theirs.append(from_core(far))
    blocks = [None] * (2 * len(PLACES))
    for (_, other_place, own), my_block, their_block in zip(PLACES, [psi, *near, far], theirs):
        blocks[own], blocks[other_place] = my_block, their_block

    partial_sum = pl.pallas_call(
        terms_kernel,
        out_shape=jax.ShapeDtypeStruct((n_x, n_z, targets * band, tile), jnp.bfloat16),
        in_specs=[smem] * 2 + [anywhere] * (2 + len(blocks)),
        out_specs=vmem,
        scratch_shapes=[
            pltpu.VMEM(left_ops.shape, left_ops.dtype),
            pltpu.VMEM(right_ops.shape, right_ops.dtype),
            pltpu.VMEM((len(blocks) * sec_dev, tile, tile), psi.dtype),
            pltpu.VMEM((targets, tile, tile), jnp.float32),
            pltpu.SemaphoreType.DMA((len(blocks) + 2,)),
        ],
        compiler_params=pltpu.CompilerParams(vmem_limit_bytes=48 * 2**20),
        name="terms",
    )(*listed, left_ops, right_ops, *blocks)

    bands = lax.all_to_all(partial_sum, "x", 0, 0, tiled=True)
    bands = lax.optimization_barrier(jnp.sum(bands.astype(jnp.float32), axis=0))
    bands = bands.astype(partial_sum.dtype)
    bands = bands.reshape(n_z * halves, sec_dev * band, tile)
    bands = lax.all_to_all(bands, ("z", "half"), 0, 0, tiled=True)
    summed = jnp.sum(bands.astype(jnp.float32), axis=0).reshape(sec_dev, band, tile)
    return local_part + summed


def solution(mesh):
    full = Mesh(mesh.devices.reshape(AXES), NAMES)
    ops, sec = ("z", "x"), ("half", "y", "core")
    in_specs = (
        P(sec, None, None),
        P(ops, None, None),
        P(ops, None, None),
        P(ops),
        P(ops, sec),
        P(ops, sec),
        P(sec, None, None),
        P(sec, None, None),
    )
    return jax.shard_map(
        per_device, mesh=full, in_specs=in_specs, out_specs=P(sec, ops, None), check_vma=False
    )
```

```python
import functools

import jax
import jax.numpy as jnp
from jax import lax
from jax.experimental import pallas as pl
from jax.experimental.pallas import tpu as pltpu
from jax.sharding import Mesh, PartitionSpec as P

AXES = (8, 4, 2, 4, 2)
NAMES = ("z", "x", "half", "y", "core")
GROUP = 4

PLACES = ((0, 1, 0), (1, 4, 2), (-1, 5, 3), (2, 7, 6))


def places_of(codes, sec_dev, core, ring, length):
    source_core = (codes // sec_dev) % 2
    away = (codes // (2 * sec_dev) - ring) * jnp.where(source_core == 0, 1, -1)
    block = jnp.full_like(codes, -1)
    for far, other, own in PLACES:
        here = (away - far) % length == 0
        block = jnp.where(here, jnp.where(source_core == core, own, other), block)
    held = jnp.logical_and(codes >= 0, block >= 0)
    return jnp.where(held, block * sec_dev + codes % sec_dev, 2 * len(PLACES) * sec_dev)


def sorted_pairs(places, weights):
    pairs = places.shape[0]
    pair = jnp.arange(pairs, dtype=jnp.int32)
    keys = places * pairs + pair
    rank = jnp.sum((keys[None, :] < keys[:, None]).astype(jnp.int32), axis=1)
    here = rank[None, :] == pair[:, None]
    listed = jnp.sum(jnp.where(here, keys[None, :], 0), axis=1)
    return listed, jnp.sum(jnp.where(here, weights[None, :], 0.0), axis=1)


def keep_kernel(block, kept_ref, sem):
    copy = pltpu.make_async_copy(block, kept_ref, sem)
    copy.start()
    copy.wait()


def terms_kernel(list_ref, weight_ref, left_hbm, right_hbm, *refs):
    blocks, (out_ref, left_ref, right_ref, tiles, sums, sems) = refs[:-6], refs[-6:]
    n_x, n_z = out_ref.shape[:2]
    targets, tile, _ = sums.shape
    band = tile // (n_x * n_z)
    pairs = list_ref.shape[0]
    sec_dev = blocks[0].shape[0]
    end = pairs * sec_dev * len(blocks)

    def fetch(b):
        return pltpu.make_async_copy(
            blocks[b], tiles.at[pl.ds(b * sec_dev, sec_dev)], sems.at[b]
        )

    operators = [
        pltpu.make_async_copy(left_hbm, left_ref, sems.at[len(blocks)]),
        pltpu.make_async_copy(right_hbm, right_ref, sems.at[len(blocks) + 1]),
    ]
    for copy in operators:
        copy.start()
    for b in range(len(blocks)):
        fetch(b).start()
    sums[...] = jnp.zeros_like(sums)
    for copy in operators:
        copy.wait()

    def more(state):
        at, _ = state
        return jnp.logical_and(at < pairs, list_ref[jnp.minimum(at, pairs - 1)] < end)

    def step(state):
        at, ready = state
        work = []
        for j in range(GROUP):
            code = list_ref[at + j]
            valid = code < end
            code = jnp.where(valid, code, 0)
            pair = lax.rem(code, pairs)
            term = lax.div(pair, targets)
            weight = jnp.where(valid, weight_ref[at + j], 0.0)
            work.append((lax.div(code, pairs), term, lax.rem(pair, targets), weight))
        needed = lax.div(functools.reduce(jnp.maximum, [w[0] for w in work]), sec_dev) + 1
        for b in range(len(blocks)):
            pl.when(jnp.logical_and(ready <= b, b < needed))(fetch(b).wait)
        def mix(place, term):
            return jnp.dot(
                left_ref[term], tiles[place], preferred_element_type=jnp.float32
            ).astype(jnp.bfloat16)

        mixed = mix(*work[0][:2])
        for j, (_, term, target, weight) in enumerate(work):
            later = mix(*work[j + 1][:2]) if j + 1 < GROUP else None
            image = jnp.dot(mixed, right_ref[term], preferred_element_type=jnp.float32)
            sums[target] += image * weight
            mixed = later
        return at + GROUP, jnp.maximum(ready, needed)

    _, ready = lax.while_loop(more, step, (0, 0))
    for b in range(len(blocks)):
        pl.when(ready <= b)(fetch(b).wait)
    for t in range(0, targets, 2):
        two = [sums[t + i].reshape(n_z, n_x, band, tile) for i in range(2)]
        rows = jnp.concatenate(two, axis=2).astype(out_ref.dtype)
        for x in range(n_x):
            out_ref[x, :, pl.ds(t * band, 2 * band), :] = rows[:, x]


def per_device(psi, left_ops, right_ops, coef, source, active, left_block, right_block):
    sec_dev, tile, _ = psi.shape
    term_dev = left_ops.shape[0]
    n_z, n_x, halves, half_y, cores = (lax.axis_size(name) for name in NAMES)
    n_ops, n_y = n_z * n_x, halves * half_y
    targets = halves * sec_dev
    pairs = term_dev * targets
    band = tile // n_ops
    ops_index = lax.axis_index("z") * n_x + lax.axis_index("x")
    core, half = lax.axis_index("core"), lax.axis_index("half")
    ring = half * half_y + lax.axis_index("y")
    smem = pl.BlockSpec(memory_space=pltpu.SMEM)
    vmem = pl.BlockSpec(memory_space=pltpu.VMEM)
    anywhere = pl.BlockSpec(memory_space=pl.ANY)

    def from_y(value, away):
        route = [(((y + a) % n_y) * 2 + c, y * 2 + c) for y in range(n_y) for c, a in ((0, away), (1, -away))]
        return lax.ppermute(value, ("half", "y", "core"), route)

    def from_core(value):
        return lax.ppermute(value, "core", [(0, 1), (1, 0)])

    near = [from_y(psi, 1), from_y(psi, -1)]
    code = jnp.where(active != 0, source, -1)
    other = from_y(code, n_y // 2)
    local_rows = lax.dynamic_slice_in_dim(psi, ops_index * band, band, 1)
    block_rows = lax.dynamic_slice_in_dim(left_block, ops_index * band, band, 1)
    local_part = jnp.einsum("tij,tjl->til", block_rows, psi, preferred_element_type=jnp.float32)
    local_part = local_part + jnp.einsum(
        "tij,tjl->til", local_rows, right_block, preferred_element_type=jnp.float32
    )

    own = pl.pallas_call(
        keep_kernel,
        out_shape=jax.ShapeDtypeStruct(psi.shape, psi.dtype),
        in_specs=[anywhere],
        out_specs=vmem,
        scratch_shapes=[pltpu.SemaphoreType.DMA],
        compiler_params=pltpu.CompilerParams(vmem_limit_bytes=48 * 2**20),
        name="keep",
    )(psi)

    near, other, local_part, psi = lax.optimization_barrier((near[::-1], other, local_part, own))
    near = near[::-1]
    far = from_y(near[0], 1)

    codes = jnp.concatenate(
        [jnp.where(half == 0, code, other), jnp.where(half == 0, other, code)], axis=1
    )
    places = places_of(codes, sec_dev, core, ring, n_y).reshape(pairs)
    listed = sorted_pairs(places, jnp.repeat(coef, targets))

    theirs = [from_core(block) for block in [psi, *near]]
    theirs, far, listed = lax.optimization_barrier((theirs[::-1], far, listed))
    theirs = theirs[::-1]
    theirs.append(from_core(far))
    blocks = [None] * (2 * len(PLACES))
    for (_, other_place, own), my_block, their_block in zip(PLACES, [psi, *near, far], theirs):
        blocks[own], blocks[other_place] = my_block, their_block

    partial_sum = pl.pallas_call(
        terms_kernel,
        out_shape=jax.ShapeDtypeStruct((n_x, n_z, targets * band, tile), jnp.bfloat16),
        in_specs=[smem] * 2 + [anywhere] * (2 + len(blocks)),
        out_specs=vmem,
        scratch_shapes=[
            pltpu.VMEM(left_ops.shape, left_ops.dtype),
            pltpu.VMEM(right_ops.shape, right_ops.dtype),
            pltpu.VMEM((len(blocks) * sec_dev, tile, tile), psi.dtype),
            pltpu.VMEM((targets, tile, tile), jnp.float32),
            pltpu.SemaphoreType.DMA((len(blocks) + 2,)),
        ],
        compiler_params=pltpu.CompilerParams(vmem_limit_bytes=48 * 2**20),
        name="terms",
    )(*listed, left_ops, right_ops, *blocks)

    bands = lax.all_to_all(partial_sum, "x", 0, 0, tiled=True)
    bands = lax.optimization_barrier(jnp.sum(bands.astype(jnp.float32), axis=0))
    bands = bands.astype(partial_sum.dtype)
    bands = bands.reshape(n_z * halves, sec_dev * band, tile)
    bands = lax.all_to_all(bands, ("z", "half"), 0, 0, tiled=True)
    summed = jnp.sum(bands.astype(jnp.float32), axis=0).reshape(sec_dev, band, tile)
    return local_part + summed


def solution(mesh):
    full = Mesh(mesh.devices.reshape(AXES), NAMES)
    ops, sec = ("z", "x"), ("half", "y", "core")
    in_specs = (
        P(sec, None, None),
        P(ops, None, None),
        P(ops, None, None),
        P(ops),
        P(ops, sec),
        P(ops, sec),
        P(sec, None, None),
        P(sec, None, None),
    )
    return jax.shard_map(
        per_device, mesh=full, in_specs=in_specs, out_specs=P(sec, ops, None), check_vma=False
    )
```
